128 devices in a mesh: ccd: 32 (over z, x, core), visit: 4 (over y).
Axes of the slice: x: 4, y: 4, z: 4, core: 2. Of those that a mesh axis runs over, the one named last changes fastest.
Arguments:
- image: bfloat16 [4, 32, 2048, 1024], P('visit', 'ccd'), may hold values from -6 to 6
- coefs: float32 [4, 32, 3], P('visit', 'ccd'), may hold values from -3 to 3
- basis_width: float32 [3], replicated, may hold values from 0.7 to 3
- psf_width: float32 [1], replicated, may hold values from 1.3 to 2.8
- warp_rows: bfloat16 [4, 32, 2048, 2048], P('visit', 'ccd'), may hold values from -1 to 2
- warp_cols: bfloat16 [4, 32, 1024, 1024], P('visit', 'ccd'), may hold values from -1 to 2
- visit_weight: int32 [4], P('visit'), may hold values from 1 to 4
- dest_patch: int32 [4, 32, 32, 1], P('visit', 'ccd'), may hold values from 0 to 31; in each aligned block of 32 rows (0 to 31, 32 to 63, ..., all dimensions but the last counted through in order) at most 2 rows name the same one
- dest_slot: int32 [4, 32, 32], P('visit', 'ccd'), may hold values from 0 to 31
Outputs:
- coadd_map: float32 [65536, 1024], P('ccd', 'visit')
- detection: float32 [65536, 1024], P('ccd', 'visit')
The draws below stay inside these ranges and needn't reach their ends.
Inputs may be any that keep to these rules, and one draw needn't show every extreme that they name: `dest_patch`: in the 32 rows of one device no patch is named more than 2 times, and in every draw some patch is named exactly 2 times by some device.
All inputs are finite; a program needn't handle non-finite values.
Results may differ from the reference program's by a relative error of at most 0.0075.
Values may be sent and summed in bfloat16 or wider, within the bound.
A program may use at most 128 MiB of HBM per device.

```python
import math
import jax
import jax.numpy as jnp
import numpy as np
from jax import lax

ROWS = 2048
COLS = 1024
BLOCKS = 32
NBASIS = 3
HALF = 10
VISITS = 4
CCDS = 32
BLOCK_ROWS = 64
CAP = 2
SKY_ROWS = 65536


def warp_table(key, side_len, source_last):
    key_shift, key_stretch, key_noise = jax.random.split(key, 3)
    offsets = jax.random.uniform(key_shift, (VISITS, CCDS, 1, 1), jnp.float32, -2.5, 2.5)
    stretch = jax.random.uniform(key_stretch, (VISITS, CCDS, 1, 1), jnp.float32, -0.003, 0.003)
    first_ids = lax.broadcasted_iota(jnp.float32, (1, 1, side_len, side_len), 2)
    second_ids = lax.broadcasted_iota(jnp.float32, (1, 1, side_len, side_len), 3)
    if source_last:
        output_ids, source_ids = (first_ids, second_ids)
    else:
        output_ids, source_ids = (second_ids, first_ids)
    target = output_ids * (1.0 + stretch) + offsets
    tent_part = jnp.maximum(0.0, 1.0 - jnp.abs(source_ids - target))
    shape_full = (VISITS, CCDS, side_len, side_len)
    noise = jax.random.normal(key_noise, shape_full, jnp.float32) * (0.5 / jnp.sqrt(side_len * 1.0))
    noise = jnp.clip(noise, -0.2, 0.2)
    return (0.8 * tent_part + noise).astype(jnp.bfloat16)


def draw_warp_rows(key, part):
    return warp_table(jax.random.fold_in(key, 11), ROWS, True)


def draw_warp_cols(key, part):
    return warp_table(jax.random.fold_in(key, 23), COLS, False)


def set_ends(result, stream_key, smallest, high):
    spot = [jax.random.randint(jax.random.fold_in(stream_key, axis), (), 0, length) for axis, length in enumerate(result.shape)]
    widest = result.shape.index(max(result.shape))
    beside = spot[:widest] + [(spot[widest] + 1) % result.shape[widest]] + spot[widest + 1:]
    return result.at[tuple(spot)].set(smallest).at[tuple(beside)].set(high)


def shard_levels(stream_key, shape, cuts, least, high):
    def one(position, parts):
        steps = jax.random.uniform(jax.random.fold_in(jax.random.fold_in(stream_key, 6), position), (parts,), jnp.float32, least / len(cuts), high / len(cuts))
        return jnp.repeat(jnp.exp(steps), shape[position] // parts).reshape((-1,) + (1,) * (len(shape) - position - 1))

    level = one(*cuts[0])
    for cut in cuts[1:]:
        level = level * one(*cut)
    return level


def assign_block(key, own, number, rows, amount, top, reach, lean):
    sequence = jax.random.permutation(key, amount)
    crowded, usual = portions_of(amount, rows * top, reach, lean, True), portions_of(amount, rows * top, reach, lean, False)
    places = jnp.arange(amount)

    def named(sizes, offset_by):
        used = int((sizes > 0).sum())
        fixed = max(1, used // 4)
        shifted = fixed + (places - fixed + offset_by * (used - fixed)) % max(1, amount - fixed)
        return jnp.zeros((amount,), jnp.int32).at[sequence[jnp.where(places < fixed, places, shifted)]].set(jnp.asarray(sizes, jnp.int32))

    sizes = jnp.where(number % 4 == 0, named(crowded, number // 4), named(usual, number - number // 4 - 1))
    mixed = jax.random.permutation(jax.random.fold_in(own, 3), amount)
    giver, taker = mixed[0:amount // 2 * 2:2], mixed[1:amount // 2 * 2:2]
    margin = jnp.minimum(sizes[giver] - 1, reach - sizes[taker]) // 2
    margin = jnp.where((giver == sequence[0]) | (taker == sequence[0]) | (sizes[taker] == 0), 0, jnp.maximum(margin, 0))
    shifted = jax.random.randint(jax.random.fold_in(own, 4), (amount // 2,), 0, 1 << 20) % (margin + 1)
    sizes = sizes.at[giver].add(-shifted).at[taker].add(shifted)
    items = jnp.searchsorted(jnp.cumsum(sizes), jnp.arange(rows * top), side="right").astype(jnp.int32)
    grid = items.reshape(top, rows).T
    grid = grid[jax.random.permutation(jax.random.fold_in(own, 1), rows)]
    offset_by = jax.random.randint(jax.random.fold_in(own, 2), (rows, 1), 0, top)
    return jnp.take_along_axis(grid, (jnp.arange(top)[None, :] + offset_by) % top, axis=1)


def portions_of(amount, total, most, slope, full):
    loads = [(1 << 20) // math.isqrt(rank ** slope) + 1 for rank in range(1, amount + 1)]
    largest = most if full else min(most, max(-(-total // amount), total * loads[0] // sum(loads)))
    least = 1 if total - largest >= amount - 1 else 0
    given, rest = [largest] + [least] * (amount - 1), total - largest - least * (amount - 1)
    while rest > 0:
        movable = [i for i in range(1, amount) if given[i] < largest] or [i for i in range(1, amount) if given[i] < most]
        mass, budget = sum([loads[i] for i in movable]), rest
        for i in movable:
            addition = min(most - given[i], max(1, budget * loads[i] // mass), rest)
            given[i] = given[i] + addition
            rest = rest - addition
    return np.array(given)


def centred(key, dims, spread, limit, pieces=(), dtype=jnp.bfloat16):
    factor_of = shard_levels(key, dims, pieces, -0.22, 0.18) if pieces else 1.0
    drawn = jax.random.normal(key, dims, jnp.float32) * spread * factor_of
    return jnp.minimum(jnp.maximum(drawn, -limit), limit).astype(dtype)


def setup_inputs(seed: int = 0) -> dict:
    key_list = jax.random.split(jax.random.key(seed), 10)
    image = centred(key_list[0], (VISITS, CCDS, ROWS, COLS), 1.0, 6.0, ((0, 4), (1, 32)))
    coefs = centred(key_list[1], (VISITS, CCDS, NBASIS), 0.6, 3.0, ((0, 4), (1, 32)), jnp.float32)
    basis_width = jnp.clip(jnp.exp(jax.random.uniform(key_list[2], (NBASIS,), jnp.float32, math.log(0.7), math.log(3.0))), 0.7, 3.0)
    psf_width = jnp.clip(jax.random.uniform(key_list[3], (1,), jnp.float32, 1.3, 2.8), 1.3, 2.8)
    warp_rows = draw_warp_rows(jax.random.fold_in(key_list[9], 71), 0)
    warp_cols = draw_warp_cols(jax.random.fold_in(key_list[9], 71), 0)
    visit_weight = set_ends(jax.random.randint(key_list[6], (VISITS,), 1, 5), jax.random.fold_in(key_list[6], 1), 1, 4).astype(jnp.int32)
    dest_patch_keys = jax.random.split(jax.random.fold_in(key_list[7], 1), VISITS * CCDS * BLOCKS // BLOCKS)
    dest_patch_turns = jax.random.permutation(jax.random.fold_in(key_list[7], 3), VISITS * CCDS * BLOCKS // BLOCKS)
    dest_patch = jax.vmap(lambda own, number: assign_block(jax.random.fold_in(key_list[7], 2), own, number, BLOCKS, CCDS, 1, CAP, 2))(dest_patch_keys, dest_patch_turns).reshape((VISITS, CCDS, BLOCKS, 1))
    dest_slot = set_ends(jax.random.randint(key_list[8], (VISITS, CCDS, BLOCKS), 0, BLOCKS), jax.random.fold_in(key_list[8], 1), 0, BLOCKS - 1).astype(jnp.int32)
    return dict(image=image, coefs=coefs, basis_width=basis_width, psf_width=psf_width, warp_rows=warp_rows, warp_cols=warp_cols, visit_weight=visit_weight, dest_patch=dest_patch, dest_slot=dest_slot)


def gauss_taps(sigma_px):
    offsets = (jnp.arange(2 * HALF + 1) - HALF).astype(jnp.float32)
    values = jnp.exp(-offsets * offsets / (2.0 * sigma_px * sigma_px))
    return values / jnp.sum(values)

def shifted_rows(padded, tap_row, length):
    running = jnp.zeros((length,) + padded.shape[1:], jnp.float32)
    for offset_tap in range(2 * HALF + 1):
        running = running + tap_row[offset_tap] * padded[offset_tap:offset_tap + length]
    return running

def shifted_cols(padded, tap_row, length):
    running = jnp.zeros((padded.shape[0], length), jnp.float32)
    for offset_tap in range(2 * HALF + 1):
        running = running + tap_row[offset_tap] * padded[:, offset_tap:offset_tap + length]
    return running

def reference(image, coefs, basis_width, psf_width, warp_rows, warp_cols, visit_weight, dest_patch, dest_slot):
    basis_taps = [lax.optimization_barrier(gauss_taps(basis_width[number]).astype(jnp.bfloat16)).astype(jnp.float32) for number in range(NBASIS)]

    def one_window(entry):
        pixels, mixing, rows_map, cols_map = entry
        padded = jnp.pad(pixels.astype(jnp.float32), ((HALF, HALF), (0, 0)))
        matched = jnp.zeros((ROWS, COLS), jnp.float32)
        for number in range(NBASIS):
            rowpass = shifted_rows(padded, basis_taps[number], ROWS).astype(jnp.bfloat16)
            widened = jnp.pad(rowpass.astype(jnp.float32), ((0, 0), (HALF, HALF)))
            matched = matched + mixing[number] * shifted_cols(widened, basis_taps[number], COLS)
        matched = matched.astype(jnp.bfloat16)
        halfway = jnp.dot(rows_map.astype(jnp.float32), matched.astype(jnp.float32)).astype(jnp.bfloat16)
        return jnp.dot(halfway.astype(jnp.float32), cols_map.astype(jnp.float32)).astype(jnp.bfloat16)
    warped = lax.map(one_window, (image.reshape(VISITS * CCDS, ROWS, COLS), coefs.reshape(VISITS * CCDS, NBASIS), warp_rows.reshape(VISITS * CCDS, ROWS, ROWS), warp_cols.reshape(VISITS * CCDS, COLS, COLS)))
    warped = warped.reshape(VISITS, CCDS * BLOCKS, BLOCK_ROWS * COLS)
    cell_ids = (dest_patch[..., 0] * BLOCKS + dest_slot).reshape(VISITS, CCDS * BLOCKS).astype(jnp.int32)
    total = jnp.zeros((CCDS * BLOCKS, BLOCK_ROWS * COLS), jnp.float32)
    coverage = jnp.zeros((CCDS * BLOCKS,), jnp.float32)
    for visit_idx in range(VISITS):
        weight = visit_weight[visit_idx].astype(jnp.float32)
        summed = jax.ops.segment_sum(warped[visit_idx].astype(jnp.float32), cell_ids[visit_idx], num_segments=CCDS * BLOCKS)
        partial_value = (weight * summed).astype(jnp.bfloat16)
        total = total + lax.optimization_barrier(partial_value).astype(jnp.float32)
        coverage = coverage + jax.ops.segment_sum(jnp.ones((CCDS * BLOCKS,), jnp.float32) * weight, cell_ids[visit_idx], num_segments=CCDS * BLOCKS)
    total = total.reshape(SKY_ROWS, COLS)
    cover_rows = jnp.repeat(coverage, BLOCK_ROWS)
    coadd_map = total / jnp.maximum(cover_rows, 1.0)[:, None]
    psf_taps = gauss_taps(psf_width[0])
    squared = psf_taps * psf_taps
    framed = jnp.pad(total, ((HALF, HALF), (HALF, HALF)))
    signal = shifted_cols(shifted_rows(framed, psf_taps, SKY_ROWS), psf_taps, COLS)
    depth_rows = shifted_rows(jnp.pad(cover_rows, (HALF, HALF)), squared, SKY_ROWS)
    depth_cols = shifted_rows(jnp.pad(jnp.ones((COLS,), jnp.float32), (HALF, HALF)), squared, COLS)
    detection = signal / jnp.sqrt(jnp.maximum(depth_rows[:, None] * depth_cols[None, :], 0.05))
    return (coadd_map, detection)
```

```python
import functools

import jax
import jax.numpy as jnp
from jax import lax
from jax.experimental import pallas as pl
from jax.experimental.pallas import tpu as pltpu
from jax.sharding import PartitionSpec as P

NBASIS = 3
HALF = 10
ROWS = 2048
COLS = 1024
BLOCKS = 32
PIECE = 64
VISITS = 4
CCDS = 32
DEVICES = VISITS * CCDS
CELLS = CCDS * BLOCKS
PIECES = DEVICES * BLOCKS
PART = COLS // VISITS
WIDE = 2 * PART
FLOOR = 0.05
VMEM_LIMIT = 60 * 1024 * 1024

F32 = jnp.float32
BF16 = jnp.bfloat16


def dot(a, b):
    return jnp.dot(a, b, preferred_element_type=F32)


def gauss_norm(two_var):
    m = lax.broadcasted_iota(jnp.int32, (1, 128), 1)
    d = (m - HALF).astype(F32)
    return jnp.sum(jnp.where(m <= 2 * HALF, jnp.exp(-d * d / two_var), 0.0), axis=1, keepdims=True)


def gauss_at(d, two_var, norm):
    df = d.astype(F32)
    return jnp.where(jnp.abs(d) <= HALF, jnp.exp(-df * df / two_var) / norm, 0.0)


def warp_kernel(coefs, widths, image, warp_rows, warp_cols, out, img, rp, matched, wr, wc, wf, rb, cb, sems):
    copies = [
        pltpu.make_async_copy(image.at[pl.ds(512 * n, 512)], img.at[pl.ds(16 + 512 * n, 512)], sems.at[n])
        for n in range(4)
    ]
    wr_copies = [
        pltpu.make_async_copy(warp_rows.at[pl.ds(512 * n, 512)], wr.at[pl.ds(512 * n, 512)], sems.at[4 + n])
        for n in range(4)
    ]
    wc_copy = pltpu.make_async_copy(warp_cols, wc, sems.at[8])
    for c in copies:
        c.start()
    for c in wr_copies[:1] + [wc_copy] + wr_copies[1:]:
        c.start()
    img[0:16, :] = jnp.zeros((16, COLS), BF16)
    img[ROWS + 16 : ROWS + 32, :] = jnp.zeros((16, COLS), BF16)
    rp[:, :, 0:128] = jnp.zeros((NBASIS, ROWS, 128), BF16)
    rp[:, :, COLS + 128 : COLS + 256] = jnp.zeros((NBASIS, ROWS, 128), BF16)
    d_row = lax.broadcasted_iota(jnp.int32, (128, 160), 1) - 16 - lax.broadcasted_iota(jnp.int32, (128, 160), 0)
    d_col = lax.broadcasted_iota(jnp.int32, (512, 256), 0) - 128 - lax.broadcasted_iota(jnp.int32, (512, 256), 1)
    for b in range(NBASIS):
        sigma = widths[b]
        two_var = 2.0 * sigma * sigma
        norm = gauss_norm(two_var)
        rb[b * 128 : (b + 1) * 128, :] = gauss_at(d_row, two_var, norm).astype(BF16)
        cb[b] = gauss_at(d_col, two_var, norm).astype(BF16)

    def row_block(n, carry):
        y = pl.multiple_of(n * 128, 128)
        res = dot(rb[...], img[pl.ds(y, 160), :]).astype(BF16)
        for b in range(NBASIS):
            rp[b, pl.ds(y, 128), 128 : COLS + 128] = res[b * 128 : (b + 1) * 128]
        return carry

    for c in copies:
        c.wait()
    lax.fori_loop(0, ROWS // 128, row_block, 0)

    def col_block(n, carry):
        y = pl.multiple_of(n * 512, 512)
        for q in range(VISITS):
            acc = coefs[0] * dot(rp[0, pl.ds(y, 512), q * 256 : q * 256 + 512], cb[0])
            for b in range(1, NBASIS):
                acc = acc + coefs[b] * dot(rp[b, pl.ds(y, 512), q * 256 : q * 256 + 512], cb[b])
            matched[pl.ds(y, 512), q * 256 : (q + 1) * 256] = acc.astype(BF16)
        return carry

    lax.fori_loop(0, ROWS // 512, col_block, 0)
    wc_copy.wait()
    for c in wr_copies:
        c.wait()

    def warp_block(n, carry):
        y = pl.multiple_of(n * 256, 256)
        halfway = dot(wr[pl.ds(y, 256), :], matched[...]).astype(BF16)
        warped = dot(halfway, wc[...])
        for l in range(COLS // 128):
            wf[l, pl.ds(y, 256), :] = warped[:, l * 128 : (l + 1) * 128]
        return carry

    for g in range(2):
        lax.fori_loop(4 * g, 4 * g + 4, warp_block, 0)

        def pack(c, carry):
            for i in range(2):
                for l in range(COLS // 128):
                    rows = wf[l, pl.ds(g * 1024 + c + 32 * i, 16, stride=PIECE), :]
                    j, h = divmod(l, 2)
                    out[c * VISITS + j, g * 16 : (g + 1) * 16, i * 256 + h * 128 : i * 256 + (h + 1) * 128] = rows.astype(BF16)
            return carry

        lax.fori_loop(0, CCDS, pack, 0)


def warp_window(coefs, widths, image, warp_rows, warp_cols):
    smem = pl.BlockSpec(memory_space=pltpu.SMEM)
    hbm = pl.BlockSpec(memory_space=pl.ANY)
    return pl.pallas_call(
        warp_kernel,
        out_shape=jax.ShapeDtypeStruct((DEVICES, BLOCKS, WIDE), BF16),
        in_specs=[smem, smem, hbm, hbm, hbm],
        out_specs=pl.BlockSpec(memory_space=pltpu.VMEM),
        scratch_shapes=[
            pltpu.VMEM((ROWS + 32, COLS), BF16),
            pltpu.VMEM((NBASIS, ROWS, COLS + 256), BF16),
            pltpu.VMEM((ROWS, COLS), BF16),
            pltpu.VMEM((ROWS, ROWS), BF16),
            pltpu.VMEM((COLS, COLS), BF16),
            pltpu.VMEM((COLS // 128, ROWS, 128), F32),
            pltpu.VMEM((NBASIS * 128, 160), BF16),
            pltpu.VMEM((NBASIS, 512, 256), BF16),
            pltpu.SemaphoreType.DMA((9,)),
        ],
        compiler_params=pltpu.CompilerParams(vmem_limit_bytes=VMEM_LIMIT),
        cost_estimate=pl.CostEstimate(flops=22_000_000_000, bytes_accessed=18 << 20, transcendentals=0),
        name="warp_window",
    )(coefs, widths, image, warp_rows, warp_cols)


def cell_sum_kernel(cells, weights, inbox, out, acc):
    n = pl.program_id(0)
    step = cells.shape[1]
    ids = lax.broadcasted_iota(jnp.int32, (CELLS, step), 0)
    placing = jnp.where(ids == cells[...], weights[...], 0.0).astype(BF16)
    part = dot(placing, inbox[...])

    @pl.when(n == 0)
    def _():
        acc[...] = part

    @pl.when(n > 0)
    def _():
        acc[...] += part

    @pl.when(n == pl.num_programs(0) - 1)
    def _():
        out[...] = acc[...].astype(BF16)


def cell_sum(cells, weights, inbox):
    step = 512
    return pl.pallas_call(
        cell_sum_kernel,
        out_shape=jax.ShapeDtypeStruct((CELLS, WIDE), BF16),
        grid=(PIECES // step,),
        in_specs=[
            pl.BlockSpec((1, step), lambda n: (0, n)),
            pl.BlockSpec((1, step), lambda n: (0, n)),
            pl.BlockSpec((step, WIDE), lambda n: (n, 0)),
        ],
        out_specs=pl.BlockSpec((CELLS, WIDE), lambda n: (0, 0)),
        scratch_shapes=[pltpu.VMEM((CELLS, WIDE), F32)],
        compiler_params=pltpu.CompilerParams(vmem_limit_bytes=VMEM_LIMIT),
        name="cell_sum",
    )(cells, weights, inbox)


def order_kernel(inbox, total, edges, buf):
    for h in range(WIDE // 128):
        for c in range(CCDS):
            buf[h, c * BLOCKS : (c + 1) * BLOCKS, :] = inbox[c, :, h * 128 : (h + 1) * 128].astype(F32)

    for s in range(BLOCKS):
        for h in range(WIDE // 128):
            i, l = divmod(h, 2)
            rows = buf[h, pl.ds(s, CCDS, stride=BLOCKS), :]
            total[s * PIECE + i * 32 : s * PIECE + (i + 1) * 32, l * 128 : (l + 1) * 128] = rows.astype(BF16)
    e = lax.broadcasted_iota(jnp.int32, (32, PART), 0)
    x = lax.broadcasted_iota(jnp.int32, (32, PART), 1)
    pick = (x == jnp.where(e < 16, e, e + PART - 32)).astype(F32).astype(BF16)
    edges[...] = lax.dot_general(pick, total[...], (((1,), (1,)), ((), ())), preferred_element_type=F32).astype(BF16)


def order_rows(inbox):
    return pl.pallas_call(
        order_kernel,
        out_shape=(jax.ShapeDtypeStruct((ROWS, PART), BF16), jax.ShapeDtypeStruct((32, ROWS), BF16)),
        scratch_shapes=[pltpu.VMEM((WIDE // 128, CCDS * BLOCKS, 128), F32)],
        compiler_params=pltpu.CompilerParams(vmem_limit_bytes=VMEM_LIMIT),
        name="order_rows",
    )(inbox)


def split_bf16(v):
    hi = v.astype(BF16)
    return hi, (v - hi.astype(F32)).astype(BF16)


def detect_kernel(place, width, cover, total, above, below, edges, coadd, detection, ext):
    column0 = place[0] * PART
    ext[0:16, 0:PART] = above[...]
    ext[16 : ROWS + 16, 0:PART] = total[...]
    ext[ROWS + 16 : ROWS + 32, 0:PART] = below[...]
    e = lax.broadcasted_iota(jnp.int32, (32, 128), 0)
    x = lax.broadcasted_iota(jnp.int32, (32, 128), 1)
    pick = (e == x).astype(F32).astype(BF16)
    ext[:, PART : PART + 128] = lax.dot_general(
        edges[...], pick, (((0,), (0,)), ((), ())), preferred_element_type=F32
    )[0 : ROWS + 32].astype(BF16)
    sigma = width[0]
    two_var = 2.0 * sigma * sigma
    norm = gauss_norm(two_var)
    d_row = lax.broadcasted_iota(jnp.int32, (128, 160), 1) - 16 - lax.broadcasted_iota(jnp.int32, (128, 160), 0)
    row_hi, row_lo = split_bf16(gauss_at(d_row, two_var, norm))
    k = lax.broadcasted_iota(jnp.int32, (PART + 128, PART), 0)
    x = lax.broadcasted_iota(jnp.int32, (PART + 128, PART), 1)
    source = jnp.where(k < PART, k, jnp.where(k < PART + 16, k - PART - 16, jnp.where(k < PART + 32, k - 16, 4 * COLS)))
    col_hi, col_lo = split_bf16(gauss_at(source - x, two_var, norm))

    xs = lax.broadcasted_iota(jnp.int32, (1, PART), 1) + column0
    zero = jnp.zeros((1, PART), F32)
    depth_cols = zero
    r = lax.broadcasted_iota(jnp.int32, (PIECE, PART), 0)
    here = jnp.zeros((PIECE, PART), F32)
    before = jnp.zeros((PIECE, PART), F32)
    after = jnp.zeros((PIECE, PART), F32)
    for m in range(2 * HALF + 1):
        d = float(m - HALF)
        tap = jnp.exp(jnp.full((1, PART), -d * d, F32) / two_var) / norm
        sq = tap * tap
        at = xs + (m - HALF)
        depth_cols = depth_cols + jnp.where((at >= 0) & (at < COLS), sq, 0.0)
        row = r + (m - HALF)
        before = before + jnp.where(row < 0, sq, 0.0)
        after = after + jnp.where(row >= PIECE, sq, 0.0)
        here = here + jnp.where((row >= 0) & (row < PIECE), sq, 0.0)

    def block(n, carry):
        y = pl.multiple_of(n * 128, 128)
        window = ext[pl.ds(y, 160), :]
        across = dot(row_hi, window) + dot(row_lo, window)
        a_hi, a_lo = split_bf16(across)
        signal = dot(a_hi, col_hi) + (dot(a_lo, col_hi) + dot(a_hi, col_lo))
        for h in range(2):
            s = n * 2 + h
            c = cover[s + 1]
            depth_rows = cover[s] * before + c * here + cover[s + 2] * after
            scale = lax.rsqrt(jnp.maximum(depth_rows * depth_cols, FLOOR))
            rows = pl.ds(pl.multiple_of(y + h * PIECE, PIECE), PIECE)
            detection[rows, :] = signal[h * PIECE : (h + 1) * PIECE] * scale
            own = ext[pl.ds(pl.multiple_of(y + h * PIECE + 16, 16), PIECE), 0:PART].astype(F32)
            coadd[rows, :] = own / jnp.maximum(jnp.full((PIECE, PART), c, F32), 1.0)
        return carry

    lax.fori_loop(0, ROWS // 128, block, 0)


def detect(place, width, cover, total, above, below, edges):
    smem = pl.BlockSpec(memory_space=pltpu.SMEM)
    vmem = pl.BlockSpec(memory_space=pltpu.VMEM)
    out = jax.ShapeDtypeStruct((ROWS, PART), F32)
    return pl.pallas_call(
        detect_kernel,
        out_shape=(out, out),
        in_specs=[smem, smem, smem, vmem, vmem, vmem, vmem],
        scratch_shapes=[pltpu.VMEM((ROWS + 32, PART + 128), BF16)],
        compiler_params=pltpu.CompilerParams(vmem_limit_bytes=VMEM_LIMIT),
        name="detect",
    )(place, width, cover, total, above, below, edges)


def local(image, coefs, basis_width, psf_width, warp_rows, warp_cols, visit_weight, dest_patch, dest_slot):
    ccd = lax.axis_index("ccd")
    visit = lax.axis_index("visit")
    cells = dest_patch.reshape(-1) * BLOCKS + dest_slot.reshape(-1)
    tagged = lax.all_gather(cells * 8 + visit_weight[0], ("ccd", "visit"), tiled=True)
    outbox = warp_window(coefs.reshape(-1), basis_width, image[0, 0], warp_rows[0, 0], warp_cols[0, 0])
    inbox = lax.all_to_all(outbox, ("ccd", "visit"), split_axis=0, concat_axis=0, tiled=True)
    all_cells = (tagged // 8).reshape(1, PIECES)
    weights = (tagged % 8).astype(F32).reshape(1, PIECES)
    summed = cell_sum(all_cells, weights, inbox.reshape(PIECES, WIDE))
    near = ccd * BLOCKS - 1 + jnp.arange(BLOCKS + 2, dtype=jnp.int32)
    cover = jnp.sum(jnp.where(all_cells == near[:, None], weights, 0.0), axis=1)
    rows_in = lax.all_to_all(summed.reshape(CCDS, BLOCKS, WIDE), "ccd", split_axis=0, concat_axis=0, tiled=True)
    total, edges = order_rows(rows_in)
    up = [(n, n + 1) for n in range(CCDS - 1)]
    down = [(n + 1, n) for n in range(CCDS - 1)]
    right = [(n, n + 1) for n in range(VISITS - 1)]
    left = [(n + 1, n) for n in range(VISITS - 1)]
    above = lax.ppermute(total[ROWS - 16 :], "ccd", up)
    below = lax.ppermute(total[:16], "ccd", down)
    edges_above = jnp.concatenate([above[:, :16], above[:, PART - 16 :]], axis=1).T
    edges_below = jnp.concatenate([below[:, :16], below[:, PART - 16 :]], axis=1).T
    pad = jnp.zeros((32, 96), BF16)
    edges = jnp.concatenate([edges_above, edges, edges_below, pad], axis=1)
    from_left = lax.ppermute(edges[16:], "visit", right)
    from_right = lax.ppermute(edges[:16], "visit", left)
    edges = jnp.concatenate([from_left, from_right], axis=0)
    return detect(visit[None], psf_width, cover, total, above, below, edges)


def solution(mesh):
    placed = (
        P("visit", "ccd", None, None),
        P("visit", "ccd", None),
        P(),
        P(),
        P("visit", "ccd", None, None),
        P("visit", "ccd", None, None),
        P("visit"),
        P("visit", "ccd", None, None),
        P("visit", "ccd", None),
    )
    return jax.shard_map(
        local,
        mesh=mesh,
        in_specs=placed,
        out_specs=(P("ccd", "visit"), P("ccd", "visit")),
        check_vma=False,
    )
```

```python
import functools

import jax
import jax.numpy as jnp
from jax import lax
from jax.experimental import pallas as pl
from jax.experimental.pallas import tpu as pltpu
from jax.sharding import PartitionSpec as P

NBASIS = 3
HALF = 10
ROWS = 2048
COLS = 1024
BLOCKS = 32
PIECE = 64
VISITS = 4
CCDS = 32
DEVICES = VISITS * CCDS
CELLS = CCDS * BLOCKS
PIECES = DEVICES * BLOCKS
PART = COLS // VISITS
WIDE = 2 * PART
FLOOR = 0.05
MESH = pl.DeviceIdType.MESH
STRIDE = PIECE + 1
GROUP = 16
GROUPS = BLOCKS // GROUP
CHUNK = 512
TAIL = ROWS + 256
VMEM_LIMIT = 60 * 1024 * 1024

F32 = jnp.float32
BF16 = jnp.bfloat16


def dot(a, b):
    return jnp.dot(a, b, preferred_element_type=F32)


def gauss_norm(two_var):
    m = lax.broadcasted_iota(jnp.int32, (1, 128), 1)
    d = (m - HALF).astype(F32)
    return jnp.sum(jnp.where(m <= 2 * HALF, jnp.exp(-d * d / two_var), 0.0), axis=1, keepdims=True)


def gauss_at(d, two_var, norm):
    df = d.astype(F32)
    return jnp.where(jnp.abs(d) <= HALF, jnp.exp(-df * df / two_var) / norm, 0.0)


def shifted(steps):
    ccd, y = lax.axis_index("ccd"), lax.axis_index("visit")
    z, x, core = ccd // 8, lax.rem(ccd // 2, 4), lax.rem(ccd, 2)
    z = lax.rem(z + steps // 32, 4)
    x = lax.rem(x + lax.rem(steps // 8, 4), 4)
    core = lax.rem(core + lax.rem(steps // 4, 2), 2)
    y = lax.rem(y + lax.rem(steps, 4), 4)
    return z * 8 + x * 2 + core, y


def partner(k):
    return shifted(lax.rem(k * 59, DEVICES))


def patch_partner(k):
    return shifted(4 * lax.rem(k * 11, CCDS))


def coadd_kernel(
    coefs, widths, tags, image, warp_rows, warp_cols, ext, cover,
    img, rp, matched, wr, wc, wf, rb, cb, outbox, inbox, tags_in, acc, sumbox, rows_in, ordered, edges, turned, above, below,
    local_sems, tag_send, tag_recv, out_send, out_recv, sum_send, sum_recv, halo_send, halo_recv,
):
    ccd, visit = lax.axis_index("ccd"), lax.axis_index("visit")
    turned[...] = jnp.zeros((32, TAIL), BF16)
    above[...] = jnp.zeros((16, PART), BF16)
    below[...] = jnp.zeros((16, PART), BF16)

    barrier = pltpu.get_barrier_semaphore()

    def greet(k, carry):
        pl.semaphore_signal(barrier, inc=1, device_id=partner(k), device_id_type=MESH)
        return carry

    bounds = [0] + [CHUNK * n + 16 for n in range(1, ROWS // CHUNK)] + [ROWS]
    image_copies = [
        pltpu.make_async_copy(
            image.at[pl.ds(a, b - a)], img.at[pl.ds(16 + a, b - a)], local_sems.at[n]
        )
        for n, (a, b) in enumerate(zip(bounds[:-1], bounds[1:]))
    ]
    wr_copies = [
        pltpu.make_async_copy(
            warp_rows.at[pl.ds(1024 * n, 1024)], wr.at[pl.ds(1024 * n, 1024)], local_sems.at[4 + n]
        )
        for n in range(2)
    ]
    wc_copy = pltpu.make_async_copy(warp_cols, wc, local_sems.at[6])
    for c in image_copies + [wr_copies[0], wc_copy, wr_copies[1]]:
        c.start()
    lax.fori_loop(1, DEVICES, greet, 0)
    img[0:16, :] = jnp.zeros((16, COLS), BF16)
    img[ROWS + 16 : ROWS + 32, :] = jnp.zeros((16, COLS), BF16)
    rp[:, :, 0:128] = jnp.zeros((NBASIS, CHUNK, 128), BF16)
    rp[:, :, COLS + 128 : COLS + 256] = jnp.zeros((NBASIS, CHUNK, 128), BF16)
    d_row = lax.broadcasted_iota(jnp.int32, (128, 160), 1) - 16 - lax.broadcasted_iota(jnp.int32, (128, 160), 0)
    d_col = lax.broadcasted_iota(jnp.int32, (512, 256), 0) - 128 - lax.broadcasted_iota(jnp.int32, (512, 256), 1)
    for b in range(NBASIS):
        sigma = widths[b]
        two_var = 2.0 * sigma * sigma
        norm = gauss_norm(two_var)
        rb[b * 128 : (b + 1) * 128, :] = gauss_at(d_row, two_var, norm).astype(BF16)
        cb[b] = gauss_at(d_col, two_var, norm).astype(BF16)

    for n in range(ROWS // CHUNK):
        image_copies[n].wait()

        def row_block(i, carry, n=n):
            y = pl.multiple_of(i * 128, 128)
            res = dot(rb[...], img[pl.ds(pl.multiple_of(n * CHUNK + y, 128), 160), :]).astype(BF16)
            for b in range(NBASIS):
                rp[b, pl.ds(y, 128), 128 : COLS + 128] = res[b * 128 : (b + 1) * 128]
            return carry

        lax.fori_loop(0, CHUNK // 128, row_block, 0)
        for q in range(VISITS):
            mixed = coefs[0] * dot(rp[0, :, q * 256 : q * 256 + 512], cb[0])
            for b in range(1, NBASIS):
                mixed = mixed + coefs[b] * dot(rp[b, :, q * 256 : q * 256 + 512], cb[b])
            matched[n * CHUNK : (n + 1) * CHUNK, q * 256 : (q + 1) * 256] = mixed.astype(BF16)

    pl.semaphore_wait(barrier, DEVICES - 1)

    def send_tags(k, carry):
        pltpu.make_async_remote_copy(
            src_ref=tags, dst_ref=tags_in.at[k], send_sem=tag_send, recv_sem=tag_recv,
            device_id=partner(k), device_id_type=MESH,
        ).start()
        return carry

    lax.fori_loop(1, DEVICES, send_tags, 0)
    tags_in[0] = tags[...]

    wc_copy.wait()
    for g in range(GROUPS):
        wr_copies[g].wait()

        def warp_block(n, carry, g=g):
            halfway = dot(wr[pl.ds(pl.multiple_of(g * 1024 + n * 256, 256), 256), :], matched[...]).astype(BF16)
            warped = dot(halfway, wc[...])
            for l in range(COLS // 128):
                for q in range(4):
                    wf[l, pl.ds((g * GROUP + n * 4 + q) * STRIDE, PIECE), :] = warped[
                        q * PIECE : (q + 1) * PIECE, l * 128 : (l + 1) * 128
                    ]
            return carry

        lax.fori_loop(0, 4, warp_block, 0)

        def pack(box, k, row, column, g=g):
            for i in range(2):
                for h in range(2):
                    rows = wf[column * 2 + h, pl.ds(g * GROUP * STRIDE + row + 32 * i, GROUP, stride=STRIDE), :]
                    box[g, pl.ds(pl.multiple_of(k * GROUP, GROUP), GROUP), (2 * i + h) * 128 : (2 * i + h + 1) * 128] = (
                        rows.astype(BF16)
                    )

        pack(inbox, 0, ccd, visit)

        def send_group(k, carry, g=g):
            to = partner(k)
            pack(outbox, k, to[0], to[1])
            rows = pl.ds(pl.multiple_of(k * GROUP, GROUP), GROUP)
            pltpu.make_async_remote_copy(
                src_ref=outbox.at[g, rows], dst_ref=inbox.at[g, rows], send_sem=out_send.at[g],
                recv_sem=out_recv.at[g, k // 16], device_id=to, device_id_type=MESH,
            ).start()
            return carry

        lax.fori_loop(1, DEVICES, send_group, 0)

    some = pl.ds(1, DEVICES - 1)
    tags_wait = pltpu.make_async_remote_copy(
        src_ref=tags_in.at[some], dst_ref=tags_in.at[some], send_sem=tag_send, recv_sem=tag_recv,
        device_id=partner(1), device_id_type=MESH,
    )
    tags_wait.wait_send()
    tags_wait.wait_recv()
    acc[...] = jnp.zeros((CELLS, WIDE), F32)
    cover[...] = jnp.zeros((40, PART), F32)
    lane = lax.broadcasted_iota(jnp.int32, (1, 128), 1) // GROUP
    cell_ids = lax.broadcasted_iota(jnp.int32, (CELLS, 256), 0)
    near_ids = lax.broadcasted_iota(jnp.int32, (40, 256), 0) + (ccd * BLOCKS - 1)
    for g in range(GROUPS):
        def sum_chunk(kb, carry, g=g):
            halves = []
            for h in range(2):
                row = jnp.zeros((1, 128), jnp.int32)
                for i in range(8):
                    row = jnp.where(lane == i, tags_in[kb * 16 + h * 8 + i, g : g + 1, :], row)
                halves.append(row)
            tag = jnp.concatenate(halves, axis=1)
            cell, weight = tag >> 3, (tag & 7).astype(F32)
            placing = jnp.where(cell_ids == cell, weight, 0.0).astype(BF16)
            cover[...] += jnp.where(near_ids == cell, weight, 0.0)
            rows = pl.ds(pl.multiple_of(kb * 256, 256), 256)
            acc[...] += dot(placing, inbox[g, rows, :])
            return carry

        for kb in range(8):
            first, last = max(1, kb * 16), (kb + 1) * 16
            rows = pl.ds(first * GROUP, (last - first) * GROUP)
            pltpu.make_async_remote_copy(
                src_ref=inbox.at[g, rows], dst_ref=inbox.at[g, rows], send_sem=out_send.at[g],
                recv_sem=out_recv.at[g, kb], device_id=partner(1), device_id_type=MESH,
            ).wait_recv()
            sum_chunk(kb, 0)
    sumbox[...] = acc[...].astype(BF16)
    cover[...] = jnp.broadcast_to(jnp.sum(cover[...], axis=1, keepdims=True), (40, PART))

    def send_sum(k, carry):
        to = patch_partner(k)
        pltpu.make_async_remote_copy(
            src_ref=sumbox.at[pl.ds(pl.multiple_of(to[0] * BLOCKS, BLOCKS), BLOCKS)], dst_ref=rows_in.at[k],
            send_sem=sum_send, recv_sem=sum_recv, device_id=to, device_id_type=MESH,
        ).start()
        return carry

    lax.fori_loop(1, CCDS, send_sum, 0)
    rows_in[0] = sumbox[pl.ds(pl.multiple_of(ccd * BLOCKS, BLOCKS), BLOCKS)]
    some = pl.ds(1, CCDS - 1)
    sums_wait = pltpu.make_async_remote_copy(
        src_ref=rows_in.at[some], dst_ref=rows_in.at[some], send_sem=sum_send, recv_sem=sum_recv,
        device_id=partner(1), device_id_type=MESH,
    )
    sums_wait.wait_recv()

    for k in range(CCDS):
        m = (k * 11) % CCDS
        z = lax.rem(ccd // 8 + (4 - m // 8), 4)
        x = lax.rem(lax.rem(ccd // 2, 4) + (4 - m // 2 % 4), 4)
        core = lax.rem(lax.rem(ccd, 2) + m % 2, 2)
        row = z * 8 + x * 2 + core
        for h in range(WIDE // 128):
            ordered[h, pl.ds(row * (BLOCKS + 1), BLOCKS), :] = rows_in[k, :, h * 128 : (h + 1) * 128].astype(F32)
    for s in range(BLOCKS):
        for h in range(WIDE // 128):
            i, l = divmod(h, 2)
            rows = ordered[h, pl.ds(s, CCDS, stride=BLOCKS + 1), :]
            y = 16 + s * PIECE + i * 32
            ext[y : y + 32, l * 128 : (l + 1) * 128] = rows.astype(BF16)

    e = lax.broadcasted_iota(jnp.int32, (32, PART), 0)
    c = lax.broadcasted_iota(jnp.int32, (32, PART), 1)
    pick = (c == jnp.where(e < 16, e + PART - 16, e - 16)).astype(F32).astype(BF16)
    edges[...] = lax.dot_general(
        pick, ext[16 : ROWS + 16, 0:PART], (((1,), (1,)), ((), ())), preferred_element_type=F32
    ).astype(BF16)
    first, last = ext.at[pl.ds(16, 16), pl.ds(0, PART)], ext.at[pl.ds(ROWS, 16), pl.ds(0, PART)]
    whole = pl.ds(128, ROWS)
    ways = [
        (1, 0, last, above),
        (-1, 0, first, below),
        (0, 1, edges.at[pl.ds(0, 16)], turned.at[pl.ds(0, 16), whole]),
        (0, -1, edges.at[pl.ds(16, 16)], turned.at[pl.ds(16, 16), whole]),
        (1, 1, edges.at[pl.ds(0, 16), pl.ds(ROWS - 128, 128)], turned.at[pl.ds(0, 16), pl.ds(0, 128)]),
        (1, -1, edges.at[pl.ds(16, 16), pl.ds(ROWS - 128, 128)], turned.at[pl.ds(16, 16), pl.ds(0, 128)]),
        (-1, 1, edges.at[pl.ds(0, 16), pl.ds(0, 128)], turned.at[pl.ds(0, 16), pl.ds(ROWS + 128, 128)]),
        (-1, -1, edges.at[pl.ds(16, 16), pl.ds(0, 128)], turned.at[pl.ds(16, 16), pl.ds(ROWS + 128, 128)]),
    ]

    def inside(c, v):
        return (c >= 0) & (c < CCDS) & (v >= 0) & (v < VISITS)

    copies = []
    for n, (dc, dv, src, dst) in enumerate(ways):
        to = (lax.rem(ccd + dc + CCDS, CCDS), lax.rem(visit + dv + VISITS, VISITS))
        copies.append(
            pltpu.make_async_remote_copy(
                src_ref=src, dst_ref=dst, send_sem=halo_send.at[n], recv_sem=halo_recv.at[n],
                device_id=to, device_id_type=MESH,
            )
        )
        pl.when(inside(ccd + dc, visit + dv))(copies[n].start)
    for n, (dc, dv, src, dst) in enumerate(ways):
        pl.when(inside(ccd - dc, visit - dv))(copies[n].wait_recv)
    ext[0:16, 0:PART] = above[...]
    ext[ROWS + 16 : ROWS + 32, 0:PART] = below[...]
    e = lax.broadcasted_iota(jnp.int32, (32, 128), 0)
    c = lax.broadcasted_iota(jnp.int32, (32, 128), 1)
    pick = (e == c).astype(F32).astype(BF16)
    ext[:, PART : PART + 128] = lax.dot_general(
        turned[...], pick, (((0,), (0,)), ((), ())), preferred_element_type=F32
    )[112 : ROWS + 144].astype(BF16)

    for n, (dc, dv, src, dst) in enumerate(ways):
        pl.when(inside(ccd + dc, visit + dv))(copies[n].wait_send)
    sums_wait.wait_send()
    for g in range(GROUPS):
        rows = pl.ds(GROUP, (DEVICES - 1) * GROUP)
        pltpu.make_async_remote_copy(
            src_ref=outbox.at[g, rows], dst_ref=outbox.at[g, rows], send_sem=out_send.at[g],
            recv_sem=out_recv.at[g, 0], device_id=partner(1), device_id_type=MESH,
        ).wait_send()


def coadd(coefs, widths, tags, image, warp_rows, warp_cols):
    smem = pl.BlockSpec(memory_space=pltpu.SMEM)
    vmem = pl.BlockSpec(memory_space=pltpu.VMEM)
    hbm = pl.BlockSpec(memory_space=pl.ANY)
    dma = pltpu.SemaphoreType.DMA
    return pl.pallas_call(
        coadd_kernel,
        out_shape=(
            jax.ShapeDtypeStruct((ROWS + 32, PART + 128), BF16),
            jax.ShapeDtypeStruct((40, PART), F32),
        ),
        in_specs=[smem, smem, vmem, hbm, hbm, hbm],
        out_specs=(vmem, vmem),
        scratch_shapes=[
            pltpu.VMEM((ROWS + 32, COLS), BF16),
            pltpu.VMEM((NBASIS, CHUNK, COLS + 256), BF16),
            pltpu.VMEM((ROWS, COLS), BF16),
            pltpu.VMEM((ROWS, ROWS), BF16),
            pltpu.VMEM((COLS, COLS), BF16),
            pltpu.VMEM((COLS // 128, BLOCKS * STRIDE, 128), F32),
            pltpu.VMEM((NBASIS * 128, 160), BF16),
            pltpu.VMEM((NBASIS, 512, 256), BF16),
            pltpu.VMEM((GROUPS, DEVICES * GROUP, WIDE), BF16),
            pltpu.VMEM((GROUPS, DEVICES * GROUP, WIDE), BF16),
            pltpu.VMEM((DEVICES, GROUPS, 128), jnp.int32),
            pltpu.VMEM((CELLS, WIDE), F32),
            pltpu.VMEM((CELLS, WIDE), BF16),
            pltpu.VMEM((CCDS, BLOCKS, WIDE), BF16),
            pltpu.VMEM((WIDE // 128, CCDS * (BLOCKS + 1), 128), F32),
            pltpu.VMEM((32, ROWS), BF16),
            pltpu.VMEM((32, TAIL), BF16),
            pltpu.VMEM((16, PART), BF16),
            pltpu.VMEM((16, PART), BF16),
            dma((7,)),
            dma,
            dma,
            dma((GROUPS,)),
            dma((GROUPS, 8)),
            dma,
            dma,
            dma((8,)),
            dma((8,)),
        ],
        compiler_params=pltpu.CompilerParams(
            vmem_limit_bytes=VMEM_LIMIT, collective_id=0, has_side_effects=True
        ),
        cost_estimate=pl.CostEstimate(flops=30_000_000_000, bytes_accessed=18 << 20, transcendentals=0),
        name="coadd",
    )(coefs, widths, tags, image, warp_rows, warp_cols)


def split_bf16(v):
    hi = v.astype(BF16)
    return hi, (v - hi.astype(F32)).astype(BF16)


def detect_kernel(place, width, cover, ext, coadd, detection):
    column0 = place[0] * PART
    sigma = width[0]
    two_var = 2.0 * sigma * sigma
    norm = gauss_norm(two_var)
    d_row = lax.broadcasted_iota(jnp.int32, (128, 160), 1) - 16 - lax.broadcasted_iota(jnp.int32, (128, 160), 0)
    row_hi, row_lo = split_bf16(gauss_at(d_row, two_var, norm))
    k = lax.broadcasted_iota(jnp.int32, (PART + 128, PART), 0)
    x = lax.broadcasted_iota(jnp.int32, (PART + 128, PART), 1)
    source = jnp.where(k < PART, k, jnp.where(k < PART + 16, k - PART - 16, jnp.where(k < PART + 32, k - 16, 4 * COLS)))
    col_hi, col_lo = split_bf16(gauss_at(source - x, two_var, norm))

    xs = lax.broadcasted_iota(jnp.int32, (1, PART), 1) + column0
    zero = jnp.zeros((1, PART), F32)
    depth_cols = zero
    r = lax.broadcasted_iota(jnp.int32, (PIECE, PART), 0)
    here = jnp.zeros((PIECE, PART), F32)
    before = jnp.zeros((PIECE, PART), F32)
    after = jnp.zeros((PIECE, PART), F32)
    for m in range(2 * HALF + 1):
        d = float(m - HALF)
        tap = jnp.exp(jnp.full((1, PART), -d * d, F32) / two_var) / norm
        sq = tap * tap
        at = xs + (m - HALF)
        depth_cols = depth_cols + jnp.where((at >= 0) & (at < COLS), sq, 0.0)
        row = r + (m - HALF)
        before = before + jnp.where(row < 0, sq, 0.0)
        after = after + jnp.where(row >= PIECE, sq, 0.0)
        here = here + jnp.where((row >= 0) & (row < PIECE), sq, 0.0)

    def block(n, carry):
        y = pl.multiple_of(n * 128, 128)
        window = ext[pl.ds(y, 160), :]
        across = dot(row_hi, window) + dot(row_lo, window)
        a_hi, a_lo = split_bf16(across)
        signal = dot(a_hi, col_hi) + (dot(a_lo, col_hi) + dot(a_hi, col_lo))
        for h in range(2):
            s = n * 2 + h
            c = cover[pl.ds(s + 1, 1), :]
            depth_rows = cover[pl.ds(s, 1), :] * before + c * here + cover[pl.ds(s + 2, 1), :] * after
            scale = lax.rsqrt(jnp.maximum(depth_rows * depth_cols, FLOOR))
            rows = pl.ds(pl.multiple_of(y + h * PIECE, PIECE), PIECE)
            detection[rows, :] = signal[h * PIECE : (h + 1) * PIECE] * scale
            own = ext[pl.ds(pl.multiple_of(y + h * PIECE + 16, 16), PIECE), 0:PART].astype(F32)
            coadd[rows, :] = own / jnp.maximum(c, 1.0)
        return carry

    lax.fori_loop(0, ROWS // 128, block, 0)


def detect(place, width, cover, ext):
    smem = pl.BlockSpec(memory_space=pltpu.SMEM)
    vmem = pl.BlockSpec(memory_space=pltpu.VMEM)
    out = jax.ShapeDtypeStruct((ROWS, PART), F32)
    return pl.pallas_call(
        detect_kernel,
        out_shape=(out, out),
        in_specs=[smem, smem, vmem, vmem],
        compiler_params=pltpu.CompilerParams(vmem_limit_bytes=VMEM_LIMIT),
        name="detect",
    )(place, width, cover, ext)


def local(image, coefs, basis_width, psf_width, warp_rows, warp_cols, visit_weight, dest_patch, dest_slot):
    cells = dest_patch.reshape(-1) * BLOCKS + dest_slot.reshape(-1)
    tags = jnp.tile((cells * 8 + visit_weight[0]).reshape(GROUPS, GROUP), (1, 128 // GROUP))
    ext, cover = coadd(coefs.reshape(-1), basis_width, tags, image[0, 0], warp_rows[0, 0], warp_cols[0, 0])
    return detect(lax.axis_index("visit")[None], psf_width, cover, ext)


def solution(mesh):
    placed = (
        P("visit", "ccd", None, None),
        P("visit", "ccd", None),
        P(),
        P(),
        P("visit", "ccd", None, None),
        P("visit", "ccd", None, None),
        P("visit"),
        P("visit", "ccd", None, None),
        P("visit", "ccd", None),
    )
    return jax.shard_map(
        local,
        mesh=mesh,
        in_specs=placed,
        out_specs=(P("ccd", "visit"), P("ccd", "visit")),
        check_vma=False,
    )
```

```python
import functools

import jax
import jax.numpy as jnp
from jax import lax
from jax.experimental import pallas as pl
from jax.experimental.pallas import tpu as pltpu
from jax.sharding import PartitionSpec as P

NBASIS = 3
HALF = 10
ROWS = 2048
COLS = 1024
BLOCKS = 32
PIECE = 64
VISITS = 4
CCDS = 32
DEVICES = VISITS * CCDS
CELLS = CCDS * BLOCKS
PIECES = DEVICES * BLOCKS
PART = COLS // VISITS
WIDE = 2 * PART
FLOOR = 0.05
MESH = pl.DeviceIdType.MESH
STEPS = 4
GROUP = PIECE // STEPS
GROUP_ROWS = BLOCKS * GROUP
STRIDE = GROUP + 1
HALF_PART = PART // 2
SOURCES = 16
CHUNK = 512
TAIL = ROWS + 256
VMEM_LIMIT = 60 * 1024 * 1024

F32 = jnp.float32
BF16 = jnp.bfloat16


def dot(a, b):
    return jnp.dot(a, b, preferred_element_type=F32)


def gauss_norm(two_var):
    m = lax.broadcasted_iota(jnp.int32, (1, 128), 1)
    d = (m - HALF).astype(F32)
    return jnp.sum(jnp.where(m <= 2 * HALF, jnp.exp(-d * d / two_var), 0.0), axis=1, keepdims=True)


def gauss_at(d, two_var, norm):
    df = d.astype(F32)
    return jnp.where(jnp.abs(d) <= HALF, jnp.exp(-df * df / two_var) / norm, 0.0)


def place():
    ccd = lax.axis_index("ccd")
    return ccd // 8, lax.rem(ccd // 2, 4), lax.rem(ccd, 2), lax.axis_index("visit")


def beyond(dz, dx, dcore, dy):
    z, x, core, y = place()
    return lax.rem(z + dz, 4), lax.rem(x + dx, 4), lax.rem(core + dcore, 2), lax.rem(y + dy, 4)


def name_of(z, x, core, y):
    return z * 8 + x * 2 + core, y


def partner(step, n):
    m = lax.rem(n * 11, 32)
    dz = m // 8
    return beyond(dz, lax.rem(step + 4 - dz, 4), lax.rem(m // 4, 2), lax.rem(m, 4))


def patch_partner(k):
    m = lax.rem(k * 11, CCDS)
    return beyond(m // 8, lax.rem(m // 2, 4), lax.rem(m, 2), 0)


def first_row(z, x, core):
    return GROUP * lax.rem(z + x, 4) + 2 * z + core


def coadd_kernel(
    coefs, widths, weight, patches, slots, image, warp_rows, warp_cols, ext, cover,
    img, rp, matched, wr, wc, halfway, wf, rb, cb, outbox, inbox, tags, tags_in, placing, acc, sumbox, rows_in, ordered,
    edges, turned, above, below,
    local_sems, tag_send, tag_recv, out_send, out_recv, sum_send, sum_recv, halo_send, halo_recv,
):
    ccd, visit = lax.axis_index("ccd"), lax.axis_index("visit")
    turned[...] = jnp.zeros((32, TAIL), BF16)
    above[...] = jnp.zeros((16, PART), BF16)
    below[...] = jnp.zeros((16, PART), BF16)

    barrier = pltpu.get_barrier_semaphore()

    def greet(k, carry):
        to = name_of(*partner(k // 32, lax.rem(k, 32)))
        pl.semaphore_signal(barrier, inc=1, device_id=to, device_id_type=MESH)
        return carry

    z, x, core, _ = place()

    bounds = [0] + [CHUNK * n + 16 for n in range(1, ROWS // CHUNK)] + [ROWS]
    image_copies = [
        pltpu.make_async_copy(
            image.at[pl.ds(a, b - a)], img.at[pl.ds(16 + a, b - a)], local_sems.at[n]
        )
        for n, (a, b) in enumerate(zip(bounds[:-1], bounds[1:]))
    ]
    wr_copies = []
    for n in range(STEPS):
        group = pl.ds(pl.multiple_of(GROUP * lax.rem(z + x + n, 4), GROUP), GROUP)
        wr_copies.append(pltpu.make_async_copy(warp_rows.at[:, group, :], wr.at[n], local_sems.at[4 + n]))
    wc_copies = [
        pltpu.make_async_copy(
            warp_cols.at[:, pl.ds(q * PART + h * HALF_PART, HALF_PART)],
            wc.at[h, :, pl.ds(q * HALF_PART, HALF_PART)],
            local_sems.at[8 + h * VISITS + q],
        )
        for h in range(2)
        for q in range(VISITS)
    ]
    for c in image_copies + wr_copies[:1] + wc_copies[:4] + wr_copies[1:] + wc_copies[4:]:
        c.start()
    lax.fori_loop(1, DEVICES, greet, 0)
    img[0:16, :] = jnp.zeros((16, COLS), BF16)
    img[ROWS + 16 : ROWS + 32, :] = jnp.zeros((16, COLS), BF16)
    rp[:, :, 0:128] = jnp.zeros((NBASIS, CHUNK, 128), BF16)
    rp[:, :, COLS + 128 : COLS + 256] = jnp.zeros((NBASIS, CHUNK, 128), BF16)
    d_row = lax.broadcasted_iota(jnp.int32, (128, 160), 1) - 16 - lax.broadcasted_iota(jnp.int32, (128, 160), 0)
    d_col = lax.broadcasted_iota(jnp.int32, (512, 256), 0) - 128 - lax.broadcasted_iota(jnp.int32, (512, 256), 1)
    for b in range(NBASIS):
        sigma = widths[b]
        two_var = 2.0 * sigma * sigma
        norm = gauss_norm(two_var)
        rb[b * 128 : (b + 1) * 128, :] = gauss_at(d_row, two_var, norm).astype(BF16)
        cb[b] = gauss_at(d_col, two_var, norm).astype(BF16)

    for n in range(ROWS // CHUNK):
        image_copies[n].wait()

        def row_block(i, carry, n=n):
            y = pl.multiple_of(i * 128, 128)
            res = dot(rb[...], img[pl.ds(pl.multiple_of(n * CHUNK + y, 128), 160), :]).astype(BF16)
            for b in range(NBASIS):
                rp[b, pl.ds(y, 128), 128 : COLS + 128] = res[b * 128 : (b + 1) * 128]
            return carry

        lax.fori_loop(0, CHUNK // 128, row_block, 0)
        for q in range(VISITS):
            mixed = coefs[0] * dot(rp[0, :, q * 256 : q * 256 + 512], cb[0])
            for b in range(1, NBASIS):
                mixed = mixed + coefs[b] * dot(rp[b, :, q * 256 : q * 256 + 512], cb[b])
            matched[n * CHUNK : (n + 1) * CHUNK, q * 256 : (q + 1) * 256] = mixed.astype(BF16)

    cells = (patches[...] * BLOCKS + slots[...]) * 8 + weight[0]
    tags[...] = jnp.concatenate([cells] * (128 // BLOCKS), axis=1)
    pl.semaphore_wait(barrier, DEVICES - 1)

    def send_tags(k, carry):
        to = name_of(*partner(k // 32, lax.rem(k, 32)))
        pltpu.make_async_remote_copy(
            src_ref=tags, dst_ref=tags_in.at[k], send_sem=tag_send, recv_sem=tag_recv,
            device_id=to, device_id_type=MESH,
        ).start()
        return carry

    lax.fori_loop(1, DEVICES, send_tags, 0)
    tags_in[0] = tags[...]

    def pack(box, h, k, to):
        row = 2 * to[0] + to[2]
        for i in range(2):
            rows = wf[to[3], pl.ds(row + 8 * i, BLOCKS, stride=STRIDE), :]
            box[h, pl.ds(pl.multiple_of(k * BLOCKS, BLOCKS), BLOCKS), i * 128 : (i + 1) * 128] = rows.astype(BF16)

    for h in range(2):
        for c in wc_copies[h * VISITS : (h + 1) * VISITS]:
            c.wait()

        def warp_step(n, carry, h=h):
            if h == 0:
                half = dot(wr[n].reshape(GROUP_ROWS, ROWS), matched[...]).astype(BF16)
                halfway[n] = half
            else:
                half = halfway[n]
            warped = dot(half, wc[h])
            for q in range(VISITS):
                for p in range(BLOCKS):
                    wf[q, pl.ds(p * STRIDE, GROUP), :] = warped[p * GROUP : (p + 1) * GROUP, q * 128 : (q + 1) * 128]

            def send(t, carry):
                k = n * 32 + t
                to = partner(n, t)
                pack(outbox, h, k, to)
                rows = pl.ds(pl.multiple_of(k * BLOCKS, BLOCKS), BLOCKS)
                pltpu.make_async_remote_copy(
                    src_ref=outbox.at[h, rows], dst_ref=inbox.at[h, rows], send_sem=out_send.at[h],
                    recv_sem=out_recv.at[h, k // SOURCES], device_id=name_of(*to), device_id_type=MESH,
                ).start()
                return carry

            lax.fori_loop(jnp.where(n == 0, 1, 0), 32, send, 0)
            return carry

        for n in range(STEPS):
            if h == 0:
                wr_copies[n].wait()
            if n == 0:
                warp_step(0, 0)
                pack(inbox, h, 0, place())
            else:
                warp_step(n, 0)

    some = pl.ds(1, DEVICES - 1)
    tags_wait = pltpu.make_async_remote_copy(
        src_ref=tags_in.at[some], dst_ref=tags_in.at[some], send_sem=tag_send, recv_sem=tag_recv,
        device_id=name_of(*partner(0, 1)), device_id_type=MESH,
    )
    tags_wait.wait_send()
    tags_wait.wait_recv()
    lane = lax.broadcasted_iota(jnp.int32, (1, 128), 1) // BLOCKS
    cell_ids = lax.broadcasted_iota(jnp.int32, (CELLS, 128), 0)
    near_ids = lax.broadcasted_iota(jnp.int32, (40, 128), 0) + (ccd * BLOCKS - 1)

    def place_some(n, covered):
        tag = tags_in[n * 4]
        for i in range(1, 4):
            tag = jnp.where(lane == i, tags_in[n * 4 + i], tag)
        cell, heavy = tag >> 3, (tag & 7).astype(F32)
        placing[n // 4, :, pl.ds(pl.multiple_of(lax.rem(n, 4) * 128, 128), 128)] = jnp.where(cell_ids == cell, heavy, 0.0).astype(BF16)
        return covered + jnp.where(near_ids == cell, heavy, 0.0)

    covered = lax.fori_loop(0, DEVICES // 4, place_some, jnp.zeros((40, 128), F32))
    cover[...] = jnp.broadcast_to(jnp.sum(covered, axis=1, keepdims=True), (40, PART))

    for h in range(2):
        for b in range(DEVICES // SOURCES):
            first, last = max(1, b * SOURCES), (b + 1) * SOURCES
            rows = pl.ds(first * BLOCKS, (last - first) * BLOCKS)
            pltpu.make_async_remote_copy(
                src_ref=inbox.at[h, rows], dst_ref=inbox.at[h, rows], send_sem=out_send.at[h],
                recv_sem=out_recv.at[h, b], device_id=name_of(*partner(0, 1)), device_id_type=MESH,
            ).wait_recv()
            part = dot(placing[b], inbox[h, b * SOURCES * BLOCKS : last * BLOCKS, :])
            if b == 0:
                acc[...] = part
            elif b < DEVICES // SOURCES - 1:
                acc[...] += part
            else:
                sumbox[h] = (acc[...] + part).astype(BF16)

        def send_sum(k, carry, h=h):
            to = name_of(*patch_partner(k))
            pltpu.make_async_remote_copy(
                src_ref=sumbox.at[h, pl.ds(pl.multiple_of(to[0] * BLOCKS, BLOCKS), BLOCKS)], dst_ref=rows_in.at[h, k],
                send_sem=sum_send.at[h], recv_sem=sum_recv.at[h], device_id=to, device_id_type=MESH,
            ).start()
            return carry

        lax.fori_loop(1, CCDS, send_sum, 0)
        rows_in[h, 0] = sumbox[h, pl.ds(pl.multiple_of(ccd * BLOCKS, BLOCKS), BLOCKS)]

    some = pl.ds(1, CCDS - 1)
    sums_waits = []
    for h in range(2):
        sums_waits.append(
            pltpu.make_async_remote_copy(
                src_ref=rows_in.at[h, some], dst_ref=rows_in.at[h, some], send_sem=sum_send.at[h],
                recv_sem=sum_recv.at[h], device_id=name_of(*partner(0, 1)), device_id_type=MESH,
            )
        )
        sums_waits[h].wait_recv()
        for k in range(CCDS):
            m = (k * 11) % CCDS
            sz, sx, score, _ = beyond((4 - m // 8) % 4, (4 - m // 2 % 4) % 4, m % 2, 0)
            row = first_row(sz, sx, score)
            for i in range(2):
                ordered[h, pl.ds((row + 8 * i) * (BLOCKS + 1), BLOCKS), :] = rows_in[
                    h, k, :, i * 128 : (i + 1) * 128
                ].astype(F32)
        for p in range(BLOCKS):
            rows = ordered[h, pl.ds(p, PIECE, stride=BLOCKS + 1), :]
            ext[16 + p * PIECE : 16 + (p + 1) * PIECE, h * 128 : (h + 1) * 128] = rows.astype(BF16)

    e = lax.broadcasted_iota(jnp.int32, (32, PART), 0)
    c = lax.broadcasted_iota(jnp.int32, (32, PART), 1)
    pick = (c == jnp.where(e < 16, e + PART - 16, e - 16)).astype(F32).astype(BF16)
    edges[...] = lax.dot_general(
        pick, ext[16 : ROWS + 16, 0:PART], (((1,), (1,)), ((), ())), preferred_element_type=F32
    ).astype(BF16)
    first, last = ext.at[pl.ds(16, 16), pl.ds(0, PART)], ext.at[pl.ds(ROWS, 16), pl.ds(0, PART)]
    whole = pl.ds(128, ROWS)
    ways = [
        (1, 0, last, above),
        (-1, 0, first, below),
        (0, 1, edges.at[pl.ds(0, 16)], turned.at[pl.ds(0, 16), whole]),
        (0, -1, edges.at[pl.ds(16, 16)], turned.at[pl.ds(16, 16), whole]),
        (1, 1, edges.at[pl.ds(0, 16), pl.ds(ROWS - 128, 128)], turned.at[pl.ds(0, 16), pl.ds(0, 128)]),
        (1, -1, edges.at[pl.ds(16, 16), pl.ds(ROWS - 128, 128)], turned.at[pl.ds(16, 16), pl.ds(0, 128)]),
        (-1, 1, edges.at[pl.ds(0, 16), pl.ds(0, 128)], turned.at[pl.ds(0, 16), pl.ds(ROWS + 128, 128)]),
        (-1, -1, edges.at[pl.ds(16, 16), pl.ds(0, 128)], turned.at[pl.ds(16, 16), pl.ds(ROWS + 128, 128)]),
    ]

    def inside(c, v):
        return (c >= 0) & (c < CCDS) & (v >= 0) & (v < VISITS)

    copies = []
    for n, (dc, dv, src, dst) in enumerate(ways):
        to = (lax.rem(ccd + dc + CCDS, CCDS), lax.rem(visit + dv + VISITS, VISITS))
        copies.append(
            pltpu.make_async_remote_copy(
                src_ref=src, dst_ref=dst, send_sem=halo_send.at[n], recv_sem=halo_recv.at[n],
                device_id=to, device_id_type=MESH,
            )
        )
        pl.when(inside(ccd + dc, visit + dv))(copies[n].start)
    for n, (dc, dv, src, dst) in enumerate(ways):
        pl.when(inside(ccd - dc, visit - dv))(copies[n].wait_recv)
    ext[0:16, 0:PART] = above[...]
    ext[ROWS + 16 : ROWS + 32, 0:PART] = below[...]
    e = lax.broadcasted_iota(jnp.int32, (32, 128), 0)
    c = lax.broadcasted_iota(jnp.int32, (32, 128), 1)
    pick = (e == c).astype(F32).astype(BF16)
    ext[:, PART : PART + 128] = lax.dot_general(
        turned[...], pick, (((0,), (0,)), ((), ())), preferred_element_type=F32
    )[112 : ROWS + 144].astype(BF16)

    for n, (dc, dv, src, dst) in enumerate(ways):
        pl.when(inside(ccd + dc, visit + dv))(copies[n].wait_send)
    for h in range(2):
        sums_waits[h].wait_send()
        rows = pl.ds(BLOCKS, (DEVICES - 1) * BLOCKS)
        pltpu.make_async_remote_copy(
            src_ref=outbox.at[h, rows], dst_ref=outbox.at[h, rows], send_sem=out_send.at[h],
            recv_sem=out_recv.at[h, 0], device_id=name_of(*partner(0, 1)), device_id_type=MESH,
        ).wait_send()


def coadd(coefs, widths, weight, patches, slots, image, warp_rows, warp_cols):
    smem = pl.BlockSpec(memory_space=pltpu.SMEM)
    vmem = pl.BlockSpec(memory_space=pltpu.VMEM)
    hbm = pl.BlockSpec(memory_space=pl.ANY)
    dma = pltpu.SemaphoreType.DMA
    return pl.pallas_call(
        coadd_kernel,
        out_shape=(
            jax.ShapeDtypeStruct((ROWS + 32, PART + 128), BF16),
            jax.ShapeDtypeStruct((40, PART), F32),
        ),
        in_specs=[smem, smem, smem, vmem, vmem, hbm, hbm, hbm],
        out_specs=(vmem, vmem),
        scratch_shapes=[
            pltpu.VMEM((ROWS + 32, COLS), BF16),
            pltpu.VMEM((NBASIS, CHUNK, COLS + 256), BF16),
            pltpu.VMEM((ROWS, COLS), BF16),
            pltpu.VMEM((STEPS, BLOCKS, GROUP, ROWS), BF16),
            pltpu.VMEM((2, COLS, COLS // 2), BF16),
            pltpu.VMEM((STEPS, GROUP_ROWS, COLS), BF16),
            pltpu.VMEM((VISITS, BLOCKS * STRIDE, 128), F32),
            pltpu.VMEM((NBASIS * 128, 160), BF16),
            pltpu.VMEM((NBASIS, 512, 256), BF16),
            pltpu.VMEM((2, PIECES, PART), BF16),
            pltpu.VMEM((2, PIECES, PART), BF16),
            pltpu.VMEM((1, 128), jnp.int32),
            pltpu.VMEM((DEVICES, 1, 128), jnp.int32),
            pltpu.VMEM((DEVICES // SOURCES, CELLS, SOURCES * BLOCKS), BF16),
            pltpu.VMEM((CELLS, PART), F32),
            pltpu.VMEM((2, CELLS, PART), BF16),
            pltpu.VMEM((2, CCDS, BLOCKS, PART), BF16),
            pltpu.VMEM((2, PIECE * (BLOCKS + 1), 128), F32),
            pltpu.VMEM((32, ROWS), BF16),
            pltpu.VMEM((32, TAIL), BF16),
            pltpu.VMEM((16, PART), BF16),
            pltpu.VMEM((16, PART), BF16),
            dma((16,)),
            dma,
            dma,
            dma((2,)),
            dma((2, DEVICES // SOURCES)),
            dma((2,)),
            dma((2,)),
            dma((8,)),
            dma((8,)),
        ],
        compiler_params=pltpu.CompilerParams(
            vmem_limit_bytes=VMEM_LIMIT, collective_id=0, has_side_effects=True
        ),
        cost_estimate=pl.CostEstimate(flops=30_000_000_000, bytes_accessed=18 << 20, transcendentals=0),
        name="coadd",
    )(coefs, widths, weight, patches, slots, image, warp_rows, warp_cols)


def split_bf16(v):
    hi = v.astype(BF16)
    return hi, (v - hi.astype(F32)).astype(BF16)


def detect_kernel(place, width, cover, ext, coadd, detection):
    column0 = place[0] * PART
    sigma = width[0]
    two_var = 2.0 * sigma * sigma
    norm = gauss_norm(two_var)
    d_row = lax.broadcasted_iota(jnp.int32, (128, 160), 1) - 16 - lax.broadcasted_iota(jnp.int32, (128, 160), 0)
    row_hi, row_lo = split_bf16(gauss_at(d_row, two_var, norm))
    k = lax.broadcasted_iota(jnp.int32, (PART + 128, PART), 0)
    x = lax.broadcasted_iota(jnp.int32, (PART + 128, PART), 1)
    source = jnp.where(k < PART, k, jnp.where(k < PART + 16, k - PART - 16, jnp.where(k < PART + 32, k - 16, 4 * COLS)))
    col_hi, col_lo = split_bf16(gauss_at(source - x, two_var, norm))

    xs = lax.broadcasted_iota(jnp.int32, (1, PART), 1) + column0
    zero = jnp.zeros((1, PART), F32)
    depth_cols = zero
    r = lax.broadcasted_iota(jnp.int32, (PIECE, PART), 0)
    here = jnp.zeros((PIECE, PART), F32)
    before = jnp.zeros((PIECE, PART), F32)
    after = jnp.zeros((PIECE, PART), F32)
    for m in range(2 * HALF + 1):
        d = float(m - HALF)
        tap = jnp.exp(jnp.full((1, PART), -d * d, F32) / two_var) / norm
        sq = tap * tap
        at = xs + (m - HALF)
        depth_cols = depth_cols + jnp.where((at >= 0) & (at < COLS), sq, 0.0)
        row = r + (m - HALF)
        before = before + jnp.where(row < 0, sq, 0.0)
        after = after + jnp.where(row >= PIECE, sq, 0.0)
        here = here + jnp.where((row >= 0) & (row < PIECE), sq, 0.0)

    def block(n, carry):
        y = pl.multiple_of(n * 128, 128)
        window = ext[pl.ds(y, 160), :]
        across = dot(row_hi, window) + dot(row_lo, window)
        a_hi, a_lo = split_bf16(across)
        signal = dot(a_hi, col_hi) + (dot(a_lo, col_hi) + dot(a_hi, col_lo))
        for h in range(2):
            s = n * 2 + h
            c = cover[pl.ds(s + 1, 1), :]
            depth_rows = cover[pl.ds(s, 1), :] * before + c * here + cover[pl.ds(s + 2, 1), :] * after
            scale = lax.rsqrt(jnp.maximum(depth_rows * depth_cols, FLOOR))
            rows = pl.ds(pl.multiple_of(y + h * PIECE, PIECE), PIECE)
            detection[rows, :] = signal[h * PIECE : (h + 1) * PIECE] * scale
            own = ext[pl.ds(pl.multiple_of(y + h * PIECE + 16, 16), PIECE), 0:PART].astype(F32)
            coadd[rows, :] = own / jnp.maximum(c, 1.0)
        return carry

    lax.fori_loop(0, ROWS // 128, block, 0)


def detect(place, width, cover, ext):
    smem = pl.BlockSpec(memory_space=pltpu.SMEM)
    vmem = pl.BlockSpec(memory_space=pltpu.VMEM)
    out = jax.ShapeDtypeStruct((ROWS, PART), F32)
    return pl.pallas_call(
        detect_kernel,
        out_shape=(out, out),
        in_specs=[smem, smem, vmem, vmem],
        compiler_params=pltpu.CompilerParams(vmem_limit_bytes=VMEM_LIMIT),
        name="detect",
    )(place, width, cover, ext)


def local(image, coefs, basis_width, psf_width, warp_rows, warp_cols, visit_weight, dest_patch, dest_slot):
    ext, cover = coadd(
        coefs.reshape(-1), basis_width, visit_weight, dest_patch.reshape(1, BLOCKS), dest_slot.reshape(1, BLOCKS),
        image[0, 0], warp_rows.reshape(BLOCKS, PIECE, ROWS), warp_cols[0, 0],
    )
    return detect(lax.axis_index("visit")[None], psf_width, cover, ext)


def solution(mesh):
    placed = (
        P("visit", "ccd", None, None),
        P("visit", "ccd", None),
        P(),
        P(),
        P("visit", "ccd", None, None),
        P("visit", "ccd", None, None),
        P("visit"),
        P("visit", "ccd", None, None),
        P("visit", "ccd", None),
    )
    return jax.shard_map(
        local,
        mesh=mesh,
        in_specs=placed,
        out_specs=(P("ccd", "visit"), P("ccd", "visit")),
        check_vma=False,
    )
```

```python
import functools

import jax
import jax.numpy as jnp
from jax import lax
from jax.experimental import pallas as pl
from jax.experimental.pallas import tpu as pltpu
from jax.sharding import PartitionSpec as P

NBASIS = 3
HALF = 10
ROWS = 2048
COLS = 1024
BLOCKS = 32
PIECE = 64
VISITS = 4
CCDS = 32
DEVICES = VISITS * CCDS
CELLS = CCDS * BLOCKS
PIECES = DEVICES * BLOCKS
PART = COLS // VISITS
WIDE = 2 * PART
FLOOR = 0.05
MESH = pl.DeviceIdType.MESH
STEPS = 4
GROUP = PIECE // STEPS
GROUP_ROWS = BLOCKS * GROUP
STRIDE = GROUP + 1
HALF_PART = PART // 2
SOURCES = 16
CHUNK = 512
DETECT_ROWS = 512
TAIL = ROWS + 256
VMEM_LIMIT = 60 * 1024 * 1024

F32 = jnp.float32
BF16 = jnp.bfloat16


def dot(a, b):
    return jnp.dot(a, b, preferred_element_type=F32)


def gauss_norm(two_var):
    m = lax.broadcasted_iota(jnp.int32, (1, 128), 1)
    d = (m - HALF).astype(F32)
    return jnp.sum(jnp.where(m <= 2 * HALF, jnp.exp(-d * d / two_var), 0.0), axis=1, keepdims=True)


def gauss_at(d, two_var, norm):
    df = d.astype(F32)
    return jnp.where(jnp.abs(d) <= HALF, jnp.exp(-df * df / two_var) / norm, 0.0)


def place():
    ccd = lax.axis_index("ccd")
    return lax.div(ccd, 8), lax.rem(lax.div(ccd, 2), 4), lax.rem(ccd, 2), lax.axis_index("visit")


def beyond(here, dz, dx, dcore, dy):
    z, x, core, y = here
    return lax.rem(z + dz, 4), lax.rem(x + dx, 4), lax.rem(core + dcore, 2), lax.rem(y + dy, 4)


def name_of(z, x, core, y):
    return z * 8 + x * 2 + core, y


def partner(here, step, n):
    m = lax.rem(n * 11, 32)
    dz = lax.div(m, 8)
    return beyond(here, dz, lax.rem(step + 4 - dz, 4), lax.rem(lax.div(m, 4), 2), lax.rem(m, 4))


def patch_partner(here, k):
    m = lax.rem(k * 11, CCDS)
    return beyond(here, lax.div(m, 8), lax.rem(lax.div(m, 2), 4), lax.rem(m, 2), 0)


def first_row(z, x, core):
    return GROUP * lax.rem(z + x, 4) + 2 * z + core


def coadd_kernel(
    coefs, widths, weight, patches, slots, image, warp_rows, warp_cols, ext, cover,
    img, rp, matched, wr, wc, halfway, wf, rb, cb, outbox, inbox, tags, tags_in, placing, acc, sumbox, rows_in, ordered,
    edges, turned, above, below,
    local_sems, tag_send, tag_recv, out_send, out_recv, sum_send, sum_recv, halo_send, halo_recv,
):
    ccd, visit = lax.axis_index("ccd"), lax.axis_index("visit")
    turned[...] = jnp.zeros((32, TAIL), BF16)
    above[...] = jnp.zeros((16, PART), BF16)
    below[...] = jnp.zeros((16, PART), BF16)

    barrier = pltpu.get_barrier_semaphore()

    def greet(k, carry):
        to = lax.rem(me + k, DEVICES)
        pl.semaphore_signal(barrier, inc=1, device_id=(lax.div(to, VISITS), lax.rem(to, VISITS)), device_id_type=MESH)
        return carry

    here = place()
    z, x, core, _ = here
    me = ccd * VISITS + visit
    other = (lax.rem(ccd + 1, CCDS), visit)

    bounds = [0] + [CHUNK * n + 16 for n in range(1, ROWS // CHUNK)] + [ROWS]
    image_copies = [
        pltpu.make_async_copy(
            image.at[pl.ds(a, b - a)], img.at[pl.ds(16 + a, b - a)], local_sems.at[n]
        )
        for n, (a, b) in enumerate(zip(bounds[:-1], bounds[1:]))
    ]
    wr_copies = []
    for n in range(STEPS):
        group = pl.ds(pl.multiple_of(GROUP * lax.rem(z + x + n, 4), GROUP), GROUP)
        wr_copies.append(pltpu.make_async_copy(warp_rows.at[:, group, :], wr.at[n], local_sems.at[4 + n]))
    wc_copies = [
        pltpu.make_async_copy(
            warp_cols.at[:, pl.ds(q * PART + h * HALF_PART, HALF_PART)],
            wc.at[h, :, pl.ds(q * HALF_PART, HALF_PART)],
            local_sems.at[8 + h * VISITS + q],
        )
        for h in range(2)
        for q in range(VISITS)
    ]
    for c in image_copies + wr_copies[:1] + wc_copies[:4] + wr_copies[1:] + wc_copies[4:]:
        c.start()
    lax.fori_loop(1, DEVICES, greet, 0)
    img[0:16, :] = jnp.zeros((16, COLS), BF16)
    img[ROWS + 16 : ROWS + 32, :] = jnp.zeros((16, COLS), BF16)
    rp[:, :, 0:128] = jnp.zeros((NBASIS, CHUNK, 128), BF16)
    rp[:, :, COLS + 128 : COLS + 256] = jnp.zeros((NBASIS, CHUNK, 128), BF16)
    d_row = lax.broadcasted_iota(jnp.int32, (128, 160), 1) - 16 - lax.broadcasted_iota(jnp.int32, (128, 160), 0)
    d_col = lax.broadcasted_iota(jnp.int32, (512, 256), 0) - 128 - lax.broadcasted_iota(jnp.int32, (512, 256), 1)
    for b in range(NBASIS):
        sigma = widths[b]
        two_var = 2.0 * sigma * sigma
        norm = gauss_norm(two_var)
        rb[b * 128 : (b + 1) * 128, :] = gauss_at(d_row, two_var, norm).astype(BF16)
        cb[b] = gauss_at(d_col, two_var, norm).astype(BF16)

    for n in range(ROWS // CHUNK):
        image_copies[n].wait()

        def row_block(i, carry, n=n):
            y = pl.multiple_of(i * 128, 128)
            res = dot(rb[...], img[pl.ds(pl.multiple_of(n * CHUNK + y, 128), 160), :]).astype(BF16)
            for b in range(NBASIS):
                rp[b, pl.ds(y, 128), 128 : COLS + 128] = res[b * 128 : (b + 1) * 128]
            return carry

        lax.fori_loop(0, CHUNK // 128, row_block, 0, unroll=True)
        for q in range(VISITS):
            mixed = coefs[0] * dot(rp[0, :, q * 256 : q * 256 + 512], cb[0])
            for b in range(1, NBASIS):
                mixed = mixed + coefs[b] * dot(rp[b, :, q * 256 : q * 256 + 512], cb[b])
            matched[n * CHUNK : (n + 1) * CHUNK, q * 256 : (q + 1) * 256] = mixed.astype(BF16)

    cells = (patches[...] * BLOCKS + slots[...]) * 8 + weight[0]
    tags[...] = jnp.concatenate([cells] * (128 // BLOCKS), axis=1)
    pl.semaphore_wait(barrier, DEVICES - 1)

    tags_in[0] = tags[...]

    def pack(box, h, k, to):
        row = 2 * to[0] + to[2]
        for i in range(2):
            rows = wf[to[3], pl.ds(row + 8 * i, BLOCKS, stride=STRIDE), :]
            box[h, pl.ds(pl.multiple_of(k * BLOCKS, BLOCKS), BLOCKS), i * 128 : (i + 1) * 128] = rows.astype(BF16)

    for h in range(2):
        for c in wc_copies[h * VISITS : (h + 1) * VISITS]:
            c.wait()

        def warp_step(n, carry, h=h):
            if h == 0:
                half = dot(wr[n].reshape(GROUP_ROWS, ROWS), matched[...]).astype(BF16)
                halfway[n] = half
            else:
                half = halfway[n]
            warped = dot(half, wc[h])
            for q in range(VISITS):
                for p in range(BLOCKS):
                    wf[q, pl.ds(p * STRIDE, GROUP), :] = warped[p * GROUP : (p + 1) * GROUP, q * 128 : (q + 1) * 128]

            def send(t, carry):
                k = n * 32 + t
                to = partner(here, n, t)
                device = name_of(*to)
                pack(outbox, h, k, to)
                rows = pl.ds(pl.multiple_of(k * BLOCKS, BLOCKS), BLOCKS)
                pltpu.make_async_remote_copy(
                    src_ref=outbox.at[h, rows], dst_ref=inbox.at[h, rows], send_sem=out_send.at[h],
                    recv_sem=out_recv.at[h, lax.div(k, SOURCES)], device_id=device, device_id_type=MESH,
                ).start()
                if h == 0:
                    pltpu.make_async_remote_copy(
                        src_ref=tags, dst_ref=tags_in.at[k], send_sem=tag_send, recv_sem=tag_recv,
                        device_id=device, device_id_type=MESH,
                    ).start()
                return carry

            lax.fori_loop(1 if n == 0 else 0, 32, send, 0)
            return carry

        for n in range(STEPS):
            if h == 0:
                wr_copies[n].wait()
            warp_step(n, 0)
            if n == 0:
                pack(inbox, h, 0, here)

    some = pl.ds(1, DEVICES - 1)
    tags_wait = pltpu.make_async_remote_copy(
        src_ref=tags_in.at[some], dst_ref=tags_in.at[some], send_sem=tag_send, recv_sem=tag_recv,
        device_id=other, device_id_type=MESH,
    )
    tags_wait.wait_send()
    tags_wait.wait_recv()
    lane = lax.broadcasted_iota(jnp.int32, (1, 128), 1) // BLOCKS
    cell_ids = lax.broadcasted_iota(jnp.int32, (CELLS, 128), 0)
    near_ids = lax.broadcasted_iota(jnp.int32, (40, 128), 0) + (ccd * BLOCKS - 1)

    def place_some(n, covered):
        tag = tags_in[n * 4]
        for i in range(1, 4):
            tag = jnp.where(lane == i, tags_in[n * 4 + i], tag)
        cell, heavy = tag >> 3, (tag & 7).astype(F32)
        placing[n // 4, :, pl.ds(pl.multiple_of(lax.rem(n, 4) * 128, 128), 128)] = jnp.where(cell_ids == cell, heavy, 0.0).astype(BF16)
        return covered + jnp.where(near_ids == cell, heavy, 0.0)

    covered = lax.fori_loop(0, DEVICES // 4, place_some, jnp.zeros((40, 128), F32))
    cover[...] = jnp.broadcast_to(jnp.sum(covered, axis=1, keepdims=True), (40, PART))

    for h in range(2):
        for b in range(DEVICES // SOURCES):
            first, last = max(1, b * SOURCES), (b + 1) * SOURCES
            rows = pl.ds(first * BLOCKS, (last - first) * BLOCKS)
            pltpu.make_async_remote_copy(
                src_ref=inbox.at[h, rows], dst_ref=inbox.at[h, rows], send_sem=out_send.at[h],
                recv_sem=out_recv.at[h, b], device_id=other, device_id_type=MESH,
            ).wait_recv()
            part = dot(placing[b], inbox[h, b * SOURCES * BLOCKS : last * BLOCKS, :])
            if b == 0:
                acc[...] = part
            elif b < DEVICES // SOURCES - 1:
                acc[...] += part
            else:
                sumbox[h] = (acc[...] + part).astype(BF16)

        def send_sum(k, carry, h=h):
            to = name_of(*patch_partner(here, k))
            pltpu.make_async_remote_copy(
                src_ref=sumbox.at[h, pl.ds(pl.multiple_of(to[0] * BLOCKS, BLOCKS), BLOCKS)], dst_ref=rows_in.at[h, k],
                send_sem=sum_send.at[h], recv_sem=sum_recv.at[h], device_id=to, device_id_type=MESH,
            ).start()
            return carry

        lax.fori_loop(1, CCDS, send_sum, 0)
        rows_in[h, 0] = sumbox[h, pl.ds(pl.multiple_of(ccd * BLOCKS, BLOCKS), BLOCKS)]

    first, last = ext.at[pl.ds(16, 16), pl.ds(0, PART)], ext.at[pl.ds(ROWS, 16), pl.ds(0, PART)]
    from_left, from_right = pl.ds(0, 16), pl.ds(16, 16)
    whole, head, tail = pl.ds(128, ROWS), pl.ds(0, 128), pl.ds(ROWS + 128, 128)
    ways = [
        (0, -1, edges.at[0], turned.at[from_right, whole]),
        (1, -1, edges.at[0, :, pl.ds(ROWS - 128, 128)], turned.at[from_right, head]),
        (-1, -1, edges.at[0, :, pl.ds(0, 128)], turned.at[from_right, tail]),
        (0, 1, edges.at[1], turned.at[from_left, whole]),
        (1, 1, edges.at[1, :, pl.ds(ROWS - 128, 128)], turned.at[from_left, head]),
        (-1, 1, edges.at[1, :, pl.ds(0, 128)], turned.at[from_left, tail]),
        (1, 0, last, above),
        (-1, 0, first, below),
    ]
    copies = []
    for n, (dc, dv, src, dst) in enumerate(ways):
        to = (lax.rem(ccd + dc + CCDS, CCDS), lax.rem(visit + dv + VISITS, VISITS))
        copies.append(
            pltpu.make_async_remote_copy(
                src_ref=src, dst_ref=dst, send_sem=halo_send.at[n], recv_sem=halo_recv.at[n],
                device_id=to, device_id_type=MESH,
            )
        )

    def inside(c, v):
        return (c >= 0) & (c < CCDS) & (v >= 0) & (v < VISITS)

    some = pl.ds(1, CCDS - 1)
    e = lax.broadcasted_iota(jnp.int32, (16, 128), 0)
    c = lax.broadcasted_iota(jnp.int32, (16, 128), 1)
    sums_waits = []
    for h in range(2):
        sums_waits.append(
            pltpu.make_async_remote_copy(
                src_ref=rows_in.at[h, some], dst_ref=rows_in.at[h, some], send_sem=sum_send.at[h],
                recv_sem=sum_recv.at[h], device_id=other, device_id_type=MESH,
            )
        )
        sums_waits[h].wait_recv()
        for k in range(CCDS):
            m = (k * 11) % CCDS
            sz, sx, score, _ = beyond(here, (4 - m // 8) % 4, (4 - m // 2 % 4) % 4, m % 2, 0)
            row = first_row(sz, sx, score)
            for i in range(2):
                ordered[h, pl.ds((row + 8 * i) * (BLOCKS + 1), BLOCKS), :] = rows_in[
                    h, k, :, i * 128 : (i + 1) * 128
                ].astype(F32)
        for p in range(BLOCKS):
            rows = ordered[h, pl.ds(p, PIECE, stride=BLOCKS + 1), :]
            ext[16 + p * PIECE : 16 + (p + 1) * PIECE, h * 128 : (h + 1) * 128] = rows.astype(BF16)
        pick = (c == e + 112 * h).astype(F32).astype(BF16)
        edges[h] = lax.dot_general(
            pick, ext[16 : ROWS + 16, h * 128 : (h + 1) * 128], (((1,), (1,)), ((), ())), preferred_element_type=F32
        ).astype(BF16)
        for n in (range(3) if h == 0 else range(3, 8)):
            dc, dv = ways[n][:2]
            pl.when(inside(ccd + dc, visit + dv))(copies[n].start)
    for n, (dc, dv, src, dst) in enumerate(ways):
        pl.when(inside(ccd - dc, visit - dv))(copies[n].wait_recv)
    ext[0:16, 0:PART] = above[...]
    ext[ROWS + 16 : ROWS + 32, 0:PART] = below[...]
    e = lax.broadcasted_iota(jnp.int32, (32, 128), 0)
    c = lax.broadcasted_iota(jnp.int32, (32, 128), 1)
    pick = (e == c).astype(F32).astype(BF16)
    ext[:, PART : PART + 128] = lax.dot_general(
        turned[...], pick, (((0,), (0,)), ((), ())), preferred_element_type=F32
    )[112 : ROWS + 144].astype(BF16)

    for n, (dc, dv, src, dst) in enumerate(ways):
        pl.when(inside(ccd + dc, visit + dv))(copies[n].wait_send)
    for h in range(2):
        sums_waits[h].wait_send()
        rows = pl.ds(BLOCKS, (DEVICES - 1) * BLOCKS)
        pltpu.make_async_remote_copy(
            src_ref=outbox.at[h, rows], dst_ref=outbox.at[h, rows], send_sem=out_send.at[h],
            recv_sem=out_recv.at[h, 0], device_id=other, device_id_type=MESH,
        ).wait_send()


def coadd(coefs, widths, weight, patches, slots, image, warp_rows, warp_cols):
    smem = pl.BlockSpec(memory_space=pltpu.SMEM)
    vmem = pl.BlockSpec(memory_space=pltpu.VMEM)
    hbm = pl.BlockSpec(memory_space=pl.ANY)
    dma = pltpu.SemaphoreType.DMA
    return pl.pallas_call(
        coadd_kernel,
        out_shape=(
            jax.ShapeDtypeStruct((ROWS + 32, PART + 128), BF16),
            jax.ShapeDtypeStruct((40, PART), F32),
        ),
        in_specs=[smem, smem, smem, vmem, vmem, hbm, hbm, hbm],
        out_specs=(vmem, vmem),
        scratch_shapes=[
            pltpu.VMEM((ROWS + 32, COLS), BF16),
            pltpu.VMEM((NBASIS, CHUNK, COLS + 256), BF16),
            pltpu.VMEM((ROWS, COLS), BF16),
            pltpu.VMEM((STEPS, BLOCKS, GROUP, ROWS), BF16),
            pltpu.VMEM((2, COLS, COLS // 2), BF16),
            pltpu.VMEM((STEPS, GROUP_ROWS, COLS), BF16),
            pltpu.VMEM((VISITS, BLOCKS * STRIDE, 128), F32),
            pltpu.VMEM((NBASIS * 128, 160), BF16),
            pltpu.VMEM((NBASIS, 512, 256), BF16),
            pltpu.VMEM((2, PIECES, PART), BF16),
            pltpu.VMEM((2, PIECES, PART), BF16),
            pltpu.VMEM((1, 128), jnp.int32),
            pltpu.VMEM((DEVICES, 1, 128), jnp.int32),
            pltpu.VMEM((DEVICES // SOURCES, CELLS, SOURCES * BLOCKS), BF16),
            pltpu.VMEM((CELLS, PART), F32),
            pltpu.VMEM((2, CELLS, PART), BF16),
            pltpu.VMEM((2, CCDS, BLOCKS, PART), BF16),
            pltpu.VMEM((2, PIECE * (BLOCKS + 1), 128), F32),
            pltpu.VMEM((2, 16, ROWS), BF16),
            pltpu.VMEM((32, TAIL), BF16),
            pltpu.VMEM((16, PART), BF16),
            pltpu.VMEM((16, PART), BF16),
            dma((16,)),
            dma,
            dma,
            dma((2,)),
            dma((2, DEVICES // SOURCES)),
            dma((2,)),
            dma((2,)),
            dma((8,)),
            dma((8,)),
        ],
        compiler_params=pltpu.CompilerParams(
            vmem_limit_bytes=VMEM_LIMIT, collective_id=0, has_side_effects=True
        ),
        cost_estimate=pl.CostEstimate(flops=30_000_000_000, bytes_accessed=18 << 20, transcendentals=0),
        name="coadd",
    )(coefs, widths, weight, patches, slots, image, warp_rows, warp_cols)


def split_bf16(v):
    hi = v.astype(BF16)
    return hi, (v - hi.astype(F32)).astype(BF16)


def detect_kernel(place, width, cover, ext, coadd, detection, rows_band, cols_band, share, depth_cols, across):
    step = pl.program_id(0)

    @pl.when(step == 0)
    def _():
        sigma = width[0]
        two_var = 2.0 * sigma * sigma
        norm = gauss_norm(two_var)
        d_row = lax.broadcasted_iota(jnp.int32, (128, 160), 1) - 16 - lax.broadcasted_iota(jnp.int32, (128, 160), 0)
        rows_band[0:128, :], rows_band[128:256, :] = split_bf16(gauss_at(d_row, two_var, norm))
        k = lax.broadcasted_iota(jnp.int32, (PART + 128, PART), 0)
        x = lax.broadcasted_iota(jnp.int32, (PART + 128, PART), 1)
        source = jnp.where(
            k < PART, k, jnp.where(k < PART + 16, k - PART - 16, jnp.where(k < PART + 32, k - 16, 4 * COLS))
        )
        cols_band[0], cols_band[1] = split_bf16(gauss_at(source - x, two_var, norm))
        xs = lax.broadcasted_iota(jnp.int32, (1, PART), 1) + place[0] * PART
        r = lax.broadcasted_iota(jnp.int32, (PIECE, 128), 0)
        columns = jnp.zeros((1, PART), F32)
        before = jnp.zeros((PIECE, 128), F32)
        after = jnp.zeros((PIECE, 128), F32)
        inner = jnp.zeros((PIECE, 128), F32)
        for m in range(2 * HALF + 1):
            d = float(m - HALF)
            tap = jnp.exp(jnp.full((1, 128), -d * d, F32) / two_var) / norm
            sq = tap * tap
            at = xs + (m - HALF)
            columns = columns + jnp.where((at >= 0) & (at < COLS), jnp.concatenate([sq, sq], axis=1), 0.0)
            row = r + (m - HALF)
            inner = inner + jnp.where((row >= 0) & (row < PIECE), sq, 0.0)
            if m < HALF:
                before = before + jnp.where(row < 0, sq, 0.0)
            if m > HALF:
                after = after + jnp.where(row >= PIECE, sq, 0.0)
        depth_cols[...] = columns
        share[0] = before
        share[1] = after
        share[2] = inner

    top = step * DETECT_ROWS
    for n in range(DETECT_ROWS // 128):
        window = ext[pl.ds(pl.multiple_of(top + n * 128, 128), 160), :]
        both = dot(rows_band[...], window)
        hi, lo = split_bf16(both[0:128] + both[128:256])
        across[0, n * 128 : (n + 1) * 128, :] = hi
        across[1, n * 128 : (n + 1) * 128, :] = lo
    signal = dot(across[0], cols_band[0]) + (dot(across[1], cols_band[0]) + dot(across[0], cols_band[1]))
    for p in range(DETECT_ROWS // PIECE):
        s = step * (DETECT_ROWS // PIECE) + p
        c = cover[pl.ds(s + 1, 1), :]
        over, under = cover[pl.ds(s, 1), :][:, 0:128], cover[pl.ds(s + 2, 1), :][:, 0:128]
        depth_rows = over * share[0] + c[:, 0:128] * share[2] + under * share[1]
        rows = slice(p * PIECE, (p + 1) * PIECE)
        for l in range(PART // 128):
            lanes = slice(l * 128, (l + 1) * 128)
            scale = lax.rsqrt(jnp.maximum(depth_rows * depth_cols[:, lanes], FLOOR))
            detection[rows, lanes] = signal[rows, lanes] * scale
        own = ext[pl.ds(pl.multiple_of(top + p * PIECE + 16, 16), PIECE), 0:PART].astype(F32)
        coadd[rows, :] = own * (1.0 / jnp.maximum(c, 1.0))


def detect(place, width, cover, ext):
    smem = pl.BlockSpec(memory_space=pltpu.SMEM)
    out = jax.ShapeDtypeStruct((ROWS, PART), F32)
    block = pl.BlockSpec((DETECT_ROWS, PART), lambda n: (n, 0))
    return pl.pallas_call(
        detect_kernel,
        out_shape=(out, out),
        grid=(ROWS // DETECT_ROWS,),
        in_specs=[
            smem,
            smem,
            pl.BlockSpec((40, PART), lambda n: (0, 0)),
            pl.BlockSpec((ROWS + 32, PART + 128), lambda n: (0, 0)),
        ],
        out_specs=(block, block),
        scratch_shapes=[
            pltpu.VMEM((256, 160), BF16),
            pltpu.VMEM((2, PART + 128, PART), BF16),
            pltpu.VMEM((3, PIECE, 128), F32),
            pltpu.VMEM((1, PART), F32),
            pltpu.VMEM((2, DETECT_ROWS, PART + 128), BF16),
        ],
        compiler_params=pltpu.CompilerParams(vmem_limit_bytes=VMEM_LIMIT),
        name="detect",
    )(place, width, cover, ext)


def local(image, coefs, basis_width, psf_width, warp_rows, warp_cols, visit_weight, dest_patch, dest_slot):
    ext, cover = coadd(
        coefs.reshape(-1), basis_width, visit_weight, dest_patch.reshape(1, BLOCKS), dest_slot.reshape(1, BLOCKS),
        image[0, 0], warp_rows.reshape(BLOCKS, PIECE, ROWS), warp_cols[0, 0],
    )
    return detect(lax.axis_index("visit")[None], psf_width, cover, ext)


def solution(mesh):
    placed = (
        P("visit", "ccd", None, None),
        P("visit", "ccd", None),
        P(),
        P(),
        P("visit", "ccd", None, None),
        P("visit", "ccd", None, None),
        P("visit"),
        P("visit", "ccd", None, None),
        P("visit", "ccd", None),
    )
    return jax.shard_map(
        local,
        mesh=mesh,
        in_specs=placed,
        out_specs=(P("ccd", "visit"), P("ccd", "visit")),
        check_vma=False,
    )
```

```python
import functools

import jax
import jax.numpy as jnp
from jax import lax
from jax.experimental import pallas as pl
from jax.experimental.pallas import tpu as pltpu
from jax.sharding import PartitionSpec as P

NBASIS = 3
HALF = 10
ROWS = 2048
COLS = 1024
BLOCKS = 32
PIECE = 64
VISITS = 4
CCDS = 32
DEVICES = VISITS * CCDS
CELLS = CCDS * BLOCKS
PIECES = DEVICES * BLOCKS
PART = COLS // VISITS
WIDE = 2 * PART
FLOOR = 0.05
MESH = pl.DeviceIdType.MESH
STEPS = 4
GROUP = PIECE // STEPS
GROUP_ROWS = BLOCKS * GROUP
STRIDE = GROUP + 1
HALF_PART = PART // 2
SOURCES = 16
CHUNK = 512
DETECT_ROWS = 512
TAIL = ROWS + 256
VMEM_LIMIT = 60 * 1024 * 1024

F32 = jnp.float32
BF16 = jnp.bfloat16


def dot(a, b):
    return jnp.dot(a, b, preferred_element_type=F32)


def gauss_norm(two_var):
    m = lax.broadcasted_iota(jnp.int32, (1, 128), 1)
    d = (m - HALF).astype(F32)
    return jnp.sum(jnp.where(m <= 2 * HALF, jnp.exp(-d * d / two_var), 0.0), axis=1, keepdims=True)


def gauss_at(d, two_var, norm):
    df = d.astype(F32)
    return jnp.where(jnp.abs(d) <= HALF, jnp.exp(-df * df / two_var) / norm, 0.0)


def place():
    ccd = lax.axis_index("ccd")
    return lax.div(ccd, 8), lax.rem(lax.div(ccd, 2), 4), lax.rem(ccd, 2), lax.axis_index("visit")


def beyond(here, dz, dx, dcore, dy):
    z, x, core, y = here
    return lax.rem(z + dz, 4), lax.rem(x + dx, 4), lax.rem(core + dcore, 2), lax.rem(y + dy, 4)


def name_of(z, x, core, y):
    return z * 8 + x * 2 + core, y


def partner(here, step, n):
    m = lax.rem(n * 21, 32)
    dz = lax.div(m, 8)
    return beyond(here, dz, lax.rem(step + 4 - dz, 4), lax.rem(lax.div(m, 4), 2), lax.rem(m, 4))


def patch_partner(here, k):
    m = lax.rem(k * 11, CCDS)
    return beyond(here, lax.div(m, 8), lax.rem(lax.div(m, 2), 4), lax.rem(m, 2), 0)


def first_row(z, x, core):
    return GROUP * lax.rem(z + x, 4) + 2 * z + core


def coadd_kernel(
    coefs, widths, weight, patches, slots, image, warp_rows, warp_cols, ext, cover,
    img, rp, matched, wr, wc, halfway, wf, rb, cb, outbox, inbox, tags, tags_in, placing, acc, sumbox, rows_in, ordered,
    edges, turned, above, below,
    local_sems, tag_send, tag_recv, out_send, out_recv, sum_send, sum_recv, halo_send, halo_recv,
):
    ccd, visit = lax.axis_index("ccd"), lax.axis_index("visit")
    turned[...] = jnp.zeros((32, TAIL), BF16)
    above[...] = jnp.zeros((16, PART), BF16)
    below[...] = jnp.zeros((16, PART), BF16)

    barrier = pltpu.get_barrier_semaphore()

    def greet(k, carry):
        to = lax.rem(me + k, DEVICES)
        pl.semaphore_signal(barrier, inc=1, device_id=(lax.div(to, VISITS), lax.rem(to, VISITS)), device_id_type=MESH)
        return carry

    here = place()
    z, x, core, _ = here
    me = ccd * VISITS + visit
    other = (lax.rem(ccd + 1, CCDS), visit)

    bounds = [0] + [CHUNK * n + 16 for n in range(1, ROWS // CHUNK)] + [ROWS]
    image_copies = [
        pltpu.make_async_copy(
            image.at[pl.ds(a, b - a)], img.at[pl.ds(16 + a, b - a)], local_sems.at[n]
        )
        for n, (a, b) in enumerate(zip(bounds[:-1], bounds[1:]))
    ]
    wr_copies = []
    for n in range(STEPS):
        group = pl.ds(pl.multiple_of(GROUP * lax.rem(z + x + n, 4), GROUP), GROUP)
        wr_copies.append(pltpu.make_async_copy(warp_rows.at[:, group, :], wr.at[n], local_sems.at[4 + n]))
    wc_copies = [
        pltpu.make_async_copy(
            warp_cols.at[:, pl.ds(q * PART + h * HALF_PART, HALF_PART)],
            wc.at[h, :, pl.ds(q * HALF_PART, HALF_PART)],
            local_sems.at[8 + h * VISITS + q],
        )
        for h in range(2)
        for q in range(VISITS)
    ]
    for c in image_copies + wr_copies[:1] + wc_copies[:4] + wr_copies[1:] + wc_copies[4:]:
        c.start()
    for k in range(1, 8):
        greet(k, 0)
    lax.fori_loop(8, DEVICES, greet, 0, unroll=8)
    img[0:16, :] = jnp.zeros((16, COLS), BF16)
    img[ROWS + 16 : ROWS + 32, :] = jnp.zeros((16, COLS), BF16)
    rp[:, :, 0:128] = jnp.zeros((NBASIS, CHUNK, 128), BF16)
    rp[:, :, COLS + 128 : COLS + 256] = jnp.zeros((NBASIS, CHUNK, 128), BF16)
    d_row = lax.broadcasted_iota(jnp.int32, (128, 160), 1) - 16 - lax.broadcasted_iota(jnp.int32, (128, 160), 0)
    d_col = lax.broadcasted_iota(jnp.int32, (160, 128), 0) - 16 - lax.broadcasted_iota(jnp.int32, (160, 128), 1)
    cb[...] = jnp.zeros((NBASIS, 512, 256), BF16)
    for b in range(NBASIS):
        sigma = widths[b]
        two_var = 2.0 * sigma * sigma
        norm = gauss_norm(two_var)
        rb[b * 128 : (b + 1) * 128, :] = gauss_at(d_row, two_var, norm).astype(BF16)
        band = gauss_at(d_col, two_var, norm).astype(BF16)
        cb[b, 112:272, 0:128] = band
        cb[b, 240:400, 128:256] = band

    for n in range(ROWS // CHUNK):
        image_copies[n].wait()

        def row_block(i, carry, n=n):
            y = pl.multiple_of(i * 128, 128)
            res = dot(rb[...], img[pl.ds(pl.multiple_of(n * CHUNK + y, 128), 160), :]).astype(BF16)
            for b in range(NBASIS):
                rp[b, pl.ds(y, 128), 128 : COLS + 128] = res[b * 128 : (b + 1) * 128]
            return carry

        lax.fori_loop(0, CHUNK // 128, row_block, 0, unroll=True)
        for q in range(VISITS):
            mixed = coefs[0] * dot(rp[0, :, q * 256 : q * 256 + 512], cb[0])
            for b in range(1, NBASIS):
                mixed = mixed + coefs[b] * dot(rp[b, :, q * 256 : q * 256 + 512], cb[b])
            matched[n * CHUNK : (n + 1) * CHUNK, q * 256 : (q + 1) * 256] = mixed.astype(BF16)

    cells = (patches[...] * BLOCKS + slots[...]) * 8 + weight[0]
    tags[...] = jnp.concatenate([cells] * (128 // BLOCKS), axis=1)
    pl.semaphore_wait(barrier, DEVICES - 1)

    tags_in[0] = tags[...]

    def pack(box, h, k, to):
        row = 2 * to[0] + to[2]
        for i in range(2):
            rows = wf[to[3], pl.ds(row + 8 * i, BLOCKS, stride=STRIDE), :]
            box[h, pl.ds(pl.multiple_of(k * BLOCKS, BLOCKS), BLOCKS), i * 128 : (i + 1) * 128] = rows.astype(BF16)

    for h in range(2):
        for c in wc_copies[h * VISITS : (h + 1) * VISITS]:
            c.wait()

        def warp_step(n, carry, h=h):
            if h == 0:
                half = dot(wr[n].reshape(GROUP_ROWS, ROWS), matched[...]).astype(BF16)
                halfway[n] = half
            else:
                half = halfway[n]
            warped = dot(half, wc[h])
            for q in range(VISITS):
                for p in range(BLOCKS):
                    wf[q, pl.ds(p * STRIDE, GROUP), :] = warped[p * GROUP : (p + 1) * GROUP, q * 128 : (q + 1) * 128]

            def send(t, carry):
                k = n * 32 + t
                to = partner(here, n, t)
                device = name_of(*to)
                pack(outbox, h, k, to)
                rows = pl.ds(pl.multiple_of(k * BLOCKS, BLOCKS), BLOCKS)
                pltpu.make_async_remote_copy(
                    src_ref=outbox.at[h, rows], dst_ref=inbox.at[h, rows], send_sem=out_send.at[h],
                    recv_sem=out_recv.at[h, lax.div(k, SOURCES)], device_id=device, device_id_type=MESH,
                ).start()
                if h == 0:
                    pltpu.make_async_remote_copy(
                        src_ref=tags, dst_ref=tags_in.at[k], send_sem=tag_send, recv_sem=tag_recv,
                        device_id=device, device_id_type=MESH,
                    ).start()
                return carry

            lax.fori_loop(1 if n == 0 else 0, 32, send, 0)
            return carry

        for n in range(STEPS):
            if h == 0:
                wr_copies[n].wait()
            warp_step(n, 0)
            if n == 0:
                pack(inbox, h, 0, here)

    some = pl.ds(1, DEVICES - 1)
    tags_wait = pltpu.make_async_remote_copy(
        src_ref=tags_in.at[some], dst_ref=tags_in.at[some], send_sem=tag_send, recv_sem=tag_recv,
        device_id=other, device_id_type=MESH,
    )
    tags_wait.wait_send()
    tags_wait.wait_recv()
    lane = lax.broadcasted_iota(jnp.int32, (1, 128), 1) // BLOCKS
    cell_ids = lax.broadcasted_iota(jnp.int32, (CELLS, 128), 0)
    near_ids = lax.broadcasted_iota(jnp.int32, (40, 128), 0) + (ccd * BLOCKS - 1)

    def place_some(n, covered):
        tag = tags_in[n * 4]
        for i in range(1, 4):
            tag = jnp.where(lane == i, tags_in[n * 4 + i], tag)
        cell, heavy = tag >> 3, (tag & 7).astype(F32)
        placing[n // 4, :, pl.ds(pl.multiple_of(lax.rem(n, 4) * 128, 128), 128)] = jnp.where(cell_ids == cell, heavy, 0.0).astype(BF16)
        return covered + jnp.where(near_ids == cell, heavy, 0.0)

    covered = lax.fori_loop(0, DEVICES // 4, place_some, jnp.zeros((40, 128), F32))
    cover[...] = jnp.broadcast_to(jnp.sum(covered, axis=1, keepdims=True), (40, PART))

    for h in range(2):
        for b in range(DEVICES // SOURCES):
            first, last = max(1, b * SOURCES), (b + 1) * SOURCES
            rows = pl.ds(first * BLOCKS, (last - first) * BLOCKS)
            pltpu.make_async_remote_copy(
                src_ref=inbox.at[h, rows], dst_ref=inbox.at[h, rows], send_sem=out_send.at[h],
                recv_sem=out_recv.at[h, b], device_id=other, device_id_type=MESH,
            ).wait_recv()
            part = dot(placing[b], inbox[h, b * SOURCES * BLOCKS : last * BLOCKS, :])
            if b == 0:
                acc[...] = part
            elif b < DEVICES // SOURCES - 1:
                acc[...] += part
            else:
                sumbox[h] = (acc[...] + part).astype(BF16)

        def send_sum(k, carry, h=h):
            to = name_of(*patch_partner(here, k))
            pltpu.make_async_remote_copy(
                src_ref=sumbox.at[h, pl.ds(pl.multiple_of(to[0] * BLOCKS, BLOCKS), BLOCKS)], dst_ref=rows_in.at[h, k],
                send_sem=sum_send.at[h], recv_sem=sum_recv.at[h], device_id=to, device_id_type=MESH,
            ).start()
            return carry

        lax.fori_loop(1, CCDS, send_sum, 0)
        rows_in[h, 0] = sumbox[h, pl.ds(pl.multiple_of(ccd * BLOCKS, BLOCKS), BLOCKS)]

    first, last = ext.at[pl.ds(16, 16), pl.ds(0, PART)], ext.at[pl.ds(ROWS, 16), pl.ds(0, PART)]
    from_left, from_right = pl.ds(0, 16), pl.ds(16, 16)
    whole, head, tail = pl.ds(128, ROWS), pl.ds(0, 128), pl.ds(ROWS + 128, 128)
    ways = [
        (0, -1, edges.at[0], turned.at[from_right, whole]),
        (1, -1, edges.at[0, :, pl.ds(ROWS - 128, 128)], turned.at[from_right, head]),
        (-1, -1, edges.at[0, :, pl.ds(0, 128)], turned.at[from_right, tail]),
        (0, 1, edges.at[1], turned.at[from_left, whole]),
        (1, 1, edges.at[1, :, pl.ds(ROWS - 128, 128)], turned.at[from_left, head]),
        (-1, 1, edges.at[1, :, pl.ds(0, 128)], turned.at[from_left, tail]),
        (1, 0, last, above),
        (-1, 0, first, below),
    ]
    copies = []
    for n, (dc, dv, src, dst) in enumerate(ways):
        to = (lax.rem(ccd + dc + CCDS, CCDS), lax.rem(visit + dv + VISITS, VISITS))
        copies.append(
            pltpu.make_async_remote_copy(
                src_ref=src, dst_ref=dst, send_sem=halo_send.at[n], recv_sem=halo_recv.at[n],
                device_id=to, device_id_type=MESH,
            )
        )

    def inside(c, v):
        return (c >= 0) & (c < CCDS) & (v >= 0) & (v < VISITS)

    some = pl.ds(1, CCDS - 1)
    e = lax.broadcasted_iota(jnp.int32, (16, 128), 0)
    c = lax.broadcasted_iota(jnp.int32, (16, 128), 1)
    sums_waits = []
    for h in range(2):
        sums_waits.append(
            pltpu.make_async_remote_copy(
                src_ref=rows_in.at[h, some], dst_ref=rows_in.at[h, some], send_sem=sum_send.at[h],
                recv_sem=sum_recv.at[h], device_id=other, device_id_type=MESH,
            )
        )
        sums_waits[h].wait_recv()
        for k in range(CCDS):
            m = (k * 11) % CCDS
            sz, sx, score, _ = beyond(here, (4 - m // 8) % 4, (4 - m // 2 % 4) % 4, m % 2, 0)
            row = first_row(sz, sx, score)
            for i in range(2):
                ordered[h, pl.ds((row + 8 * i) * (BLOCKS + 1), BLOCKS), :] = rows_in[
                    h, k, :, i * 128 : (i + 1) * 128
                ].astype(F32)
        for p in range(BLOCKS):
            rows = ordered[h, pl.ds(p, PIECE, stride=BLOCKS + 1), :]
            ext[16 + p * PIECE : 16 + (p + 1) * PIECE, h * 128 : (h + 1) * 128] = rows.astype(BF16)
        pick = (c == e + 112 * h).astype(F32).astype(BF16)
        edges[h] = lax.dot_general(
            pick, ext[16 : ROWS + 16, h * 128 : (h + 1) * 128], (((1,), (1,)), ((), ())), preferred_element_type=F32
        ).astype(BF16)
        for n in (range(3) if h == 0 else range(3, 8)):
            dc, dv = ways[n][:2]
            pl.when(inside(ccd + dc, visit + dv))(copies[n].start)
    for n, (dc, dv, src, dst) in enumerate(ways):
        pl.when(inside(ccd - dc, visit - dv))(copies[n].wait_recv)
    ext[0:16, 0:PART] = above[...]
    ext[ROWS + 16 : ROWS + 32, 0:PART] = below[...]
    e = lax.broadcasted_iota(jnp.int32, (32, 128), 0)
    c = lax.broadcasted_iota(jnp.int32, (32, 128), 1)
    pick = (e == c).astype(F32).astype(BF16)
    ext[:, PART : PART + 128] = lax.dot_general(
        turned[...], pick, (((0,), (0,)), ((), ())), preferred_element_type=F32
    )[112 : ROWS + 144].astype(BF16)

    for n, (dc, dv, src, dst) in enumerate(ways):
        pl.when(inside(ccd + dc, visit + dv))(copies[n].wait_send)
    for h in range(2):
        sums_waits[h].wait_send()
        rows = pl.ds(BLOCKS, (DEVICES - 1) * BLOCKS)
        pltpu.make_async_remote_copy(
            src_ref=outbox.at[h, rows], dst_ref=outbox.at[h, rows], send_sem=out_send.at[h],
            recv_sem=out_recv.at[h, 0], device_id=other, device_id_type=MESH,
        ).wait_send()


def coadd(coefs, widths, weight, patches, slots, image, warp_rows, warp_cols):
    smem = pl.BlockSpec(memory_space=pltpu.SMEM)
    vmem = pl.BlockSpec(memory_space=pltpu.VMEM)
    hbm = pl.BlockSpec(memory_space=pl.ANY)
    dma = pltpu.SemaphoreType.DMA
    return pl.pallas_call(
        coadd_kernel,
        out_shape=(
            jax.ShapeDtypeStruct((ROWS + 32, PART + 128), BF16),
            jax.ShapeDtypeStruct((40, PART), F32),
        ),
        in_specs=[smem, smem, smem, vmem, vmem, hbm, hbm, hbm],
        out_specs=(vmem, vmem),
        scratch_shapes=[
            pltpu.VMEM((ROWS + 32, COLS), BF16),
            pltpu.VMEM((NBASIS, CHUNK, COLS + 256), BF16),
            pltpu.VMEM((ROWS, COLS), BF16),
            pltpu.VMEM((STEPS, BLOCKS, GROUP, ROWS), BF16),
            pltpu.VMEM((2, COLS, COLS // 2), BF16),
            pltpu.VMEM((STEPS, GROUP_ROWS, COLS), BF16),
            pltpu.VMEM((VISITS, BLOCKS * STRIDE, 128), F32),
            pltpu.VMEM((NBASIS * 128, 160), BF16),
            pltpu.VMEM((NBASIS, 512, 256), BF16),
            pltpu.VMEM((2, PIECES, PART), BF16),
            pltpu.VMEM((2, PIECES, PART), BF16),
            pltpu.VMEM((1, 128), jnp.int32),
            pltpu.VMEM((DEVICES, 1, 128), jnp.int32),
            pltpu.VMEM((DEVICES // SOURCES, CELLS, SOURCES * BLOCKS), BF16),
            pltpu.VMEM((CELLS, PART), F32),
            pltpu.VMEM((2, CELLS, PART), BF16),
            pltpu.VMEM((2, CCDS, BLOCKS, PART), BF16),
            pltpu.VMEM((2, PIECE * (BLOCKS + 1), 128), F32),
            pltpu.VMEM((2, 16, ROWS), BF16),
            pltpu.VMEM((32, TAIL), BF16),
            pltpu.VMEM((16, PART), BF16),
            pltpu.VMEM((16, PART), BF16),
            dma((16,)),
            dma,
            dma,
            dma((2,)),
            dma((2, DEVICES // SOURCES)),
            dma((2,)),
            dma((2,)),
            dma((8,)),
            dma((8,)),
        ],
        compiler_params=pltpu.CompilerParams(
            vmem_limit_bytes=VMEM_LIMIT, collective_id=0, has_side_effects=True
        ),
        cost_estimate=pl.CostEstimate(flops=30_000_000_000, bytes_accessed=18 << 20, transcendentals=0),
        name="coadd",
    )(coefs, widths, weight, patches, slots, image, warp_rows, warp_cols)


def split_bf16(v):
    hi = v.astype(BF16)
    return hi, (v - hi.astype(F32)).astype(BF16)


def detect_kernel(place, width, cover, ext, coadd, detection, rows_band, cols_band, share, depth_cols, across):
    step = pl.program_id(0)

    @pl.when(step == 0)
    def _():
        sigma = width[0]
        two_var = 2.0 * sigma * sigma
        norm = gauss_norm(two_var)
        d_row = lax.broadcasted_iota(jnp.int32, (128, 160), 1) - 16 - lax.broadcasted_iota(jnp.int32, (128, 160), 0)
        rows_band[0:128, :], rows_band[128:256, :] = split_bf16(gauss_at(d_row, two_var, norm))
        k = lax.broadcasted_iota(jnp.int32, (PART + 128, PART), 0)
        x = lax.broadcasted_iota(jnp.int32, (PART + 128, PART), 1)
        source = jnp.where(
            k < PART, k, jnp.where(k < PART + 16, k - PART - 16, jnp.where(k < PART + 32, k - 16, 4 * COLS))
        )
        cols_band[0], cols_band[1] = split_bf16(gauss_at(source - x, two_var, norm))
        xs = lax.broadcasted_iota(jnp.int32, (1, PART), 1) + place[0] * PART
        r = lax.broadcasted_iota(jnp.int32, (PIECE, 128), 0)
        columns = jnp.zeros((1, PART), F32)
        before = jnp.zeros((PIECE, 128), F32)
        after = jnp.zeros((PIECE, 128), F32)
        inner = jnp.zeros((PIECE, 128), F32)
        for m in range(2 * HALF + 1):
            d = float(m - HALF)
            tap = jnp.exp(jnp.full((1, 128), -d * d, F32) / two_var) / norm
            sq = tap * tap
            at = xs + (m - HALF)
            columns = columns + jnp.where((at >= 0) & (at < COLS), jnp.concatenate([sq, sq], axis=1), 0.0)
            row = r + (m - HALF)
            inner = inner + jnp.where((row >= 0) & (row < PIECE), sq, 0.0)
            if m < HALF:
                before = before + jnp.where(row < 0, sq, 0.0)
            if m > HALF:
                after = after + jnp.where(row >= PIECE, sq, 0.0)
        depth_cols[...] = columns
        share[0] = before
        share[1] = after
        share[2] = inner

    top = step * DETECT_ROWS
    for n in range(DETECT_ROWS // 128):
        window = ext[pl.ds(pl.multiple_of(top + n * 128, 128), 160), :]
        both = dot(rows_band[...], window)
        hi, lo = split_bf16(both[0:128] + both[128:256])
        across[0, n * 128 : (n + 1) * 128, :] = hi
        across[1, n * 128 : (n + 1) * 128, :] = lo
    signal = dot(across[0], cols_band[0]) + (dot(across[1], cols_band[0]) + dot(across[0], cols_band[1]))
    for p in range(DETECT_ROWS // PIECE):
        s = step * (DETECT_ROWS // PIECE) + p
        c = cover[pl.ds(s + 1, 1), :]
        over, under = cover[pl.ds(s, 1), :][:, 0:128], cover[pl.ds(s + 2, 1), :][:, 0:128]
        depth_rows = over * share[0] + c[:, 0:128] * share[2] + under * share[1]
        rows = slice(p * PIECE, (p + 1) * PIECE)
        for l in range(PART // 128):
            lanes = slice(l * 128, (l + 1) * 128)
            scale = lax.rsqrt(jnp.maximum(depth_rows * depth_cols[:, lanes], FLOOR))
            detection[rows, lanes] = signal[rows, lanes] * scale
        own = ext[pl.ds(pl.multiple_of(top + p * PIECE + 16, 16), PIECE), 0:PART].astype(F32)
        coadd[rows, :] = own * (1.0 / jnp.maximum(c, 1.0))


def detect(place, width, cover, ext):
    smem = pl.BlockSpec(memory_space=pltpu.SMEM)
    out = jax.ShapeDtypeStruct((ROWS, PART), F32)
    block = pl.BlockSpec((DETECT_ROWS, PART), lambda n: (n, 0))
    return pl.pallas_call(
        detect_kernel,
        out_shape=(out, out),
        grid=(ROWS // DETECT_ROWS,),
        in_specs=[
            smem,
            smem,
            pl.BlockSpec((40, PART), lambda n: (0, 0)),
            pl.BlockSpec((ROWS + 32, PART + 128), lambda n: (0, 0)),
        ],
        out_specs=(block, block),
        scratch_shapes=[
            pltpu.VMEM((256, 160), BF16),
            pltpu.VMEM((2, PART + 128, PART), BF16),
            pltpu.VMEM((3, PIECE, 128), F32),
            pltpu.VMEM((1, PART), F32),
            pltpu.VMEM((2, DETECT_ROWS, PART + 128), BF16),
        ],
        compiler_params=pltpu.CompilerParams(vmem_limit_bytes=VMEM_LIMIT),
        name="detect",
    )(place, width, cover, ext)


def local(image, coefs, basis_width, psf_width, warp_rows, warp_cols, visit_weight, dest_patch, dest_slot):
    ext, cover = coadd(
        coefs.reshape(-1), basis_width, visit_weight, dest_patch.reshape(1, BLOCKS), dest_slot.reshape(1, BLOCKS),
        image[0, 0], warp_rows.reshape(BLOCKS, PIECE, ROWS), warp_cols[0, 0],
    )
    return detect(lax.axis_index("visit")[None], psf_width, cover, ext)


def solution(mesh):
    placed = (
        P("visit", "ccd", None, None),
        P("visit", "ccd", None),
        P(),
        P(),
        P("visit", "ccd", None, None),
        P("visit", "ccd", None, None),
        P("visit"),
        P("visit", "ccd", None, None),
        P("visit", "ccd", None),
    )
    return jax.shard_map(
        local,
        mesh=mesh,
        in_specs=placed,
        out_specs=(P("ccd", "visit"), P("ccd", "visit")),
        check_vma=False,
    )
```
